128 devices in a mesh: group: 32 (over z, y, x_hi), tile: 4 (over x_lo, core).
Axes of the slice: x: 4 (x_hi: 2, x_lo: 2; x = x_hi * 2 + x_lo), y: 4, z: 4, core: 2. Of those that a mesh axis runs over, the one named last changes fastest.
Arguments:
- queries: bfloat16 [16384, 2560], P(('group', 'tile')), may hold values from -100 to 100
- keys: bfloat16 [16384, 2560], P(('group', 'tile')), may hold values from -4.5 to 4.5
- values: bfloat16 [16384, 2560], P(('group', 'tile')), may hold values from -8 to 8
- cotangent: bfloat16 [16384, 2560], P(('group', 'tile')), may hold values from -6 to 6
- window: int32 [20], replicated, may hold values from 1 to 32, as said below
Outputs:
- attended: bfloat16 [16384, 2560], P(('group', 'tile'))
- grad_queries: bfloat16 [16384, 2560], P(('group', 'tile'))
- grad_keys: bfloat16 [16384, 2560], P(('group', 'tile'))
- grad_values: bfloat16 [16384, 2560], P(('group', 'tile'))
The draws below stay inside these ranges and needn't reach their ends.
Inputs may be any that keep to these rules, and one draw needn't show every extreme that they name: Some head has window 32.
All inputs are finite; a program needn't handle non-finite values.
Results may differ from the reference program's by a relative error of at most 0.04.
Values may be sent and summed in bfloat16 or wider, within the bound.
No kernel may reach another device: no remote copies, remote signals or barrier semaphores. Data moves between devices by JAX's collectives and lax.ppermute only.
A program may use at most 128 MiB of HBM per device.

```python
import jax
import jax.numpy as jnp
from jax import lax

HEADS = 20
HEAD_DIM = 128
TILE_TOK = 128
HALO = 32
PAST = 8
FRAME_TOK = 512
TOKENS = 16384
N_GROUP = 32
N_TILE = 4


def base_keys(key):
    return jax.random.truncated_normal(jax.random.fold_in(key, 101), -4.0, 4.0, (TOKENS, HEADS * HEAD_DIM), jnp.float32)


def draw_keys(key, part):
    drawn = base_keys(key)
    return drawn.astype(jnp.bfloat16)


def draw_queries(key, part):
    drawn = 2.0 * jax.random.truncated_normal(jax.random.fold_in(key, 103), -4.0, 4.0, (TOKENS, HEADS * HEAD_DIM), jnp.float32)
    return drawn.astype(jnp.bfloat16)


def draw_window(key, part):
    radius = jax.random.randint(key, (HEADS,), 1, HALO + 1)
    chosen = jax.random.randint(jax.random.fold_in(key, 7), (), 0, HEADS)
    return jnp.where(jnp.arange(HEADS) == chosen, HALO, radius).astype(jnp.int32)


def levels(stream_key, shape, pieces, low, largest):
    gain = 1.0
    for dim, parts in pieces:
        draws = jax.random.uniform(jax.random.fold_in(jax.random.fold_in(stream_key, 6), dim), (parts,), jnp.float32, low / len(pieces), largest / len(pieces))
        gain = gain * jnp.repeat(jnp.exp(draws), shape[dim] // parts).reshape((-1,) + (1,) * (len(shape) - 1 - dim))
    return gain


def gaussian(own_key, shape, scale, limit, cuts=(), dtype=jnp.bfloat16):
    values = jax.random.normal(own_key, shape, jnp.float32) * scale
    if len(cuts) > 0:
        values = levels(own_key, shape, cuts, -0.22, 0.18) * values
    return jnp.clip(values, min=-limit, max=limit).astype(dtype)


def setup_inputs(seed: int = 0) -> dict:
    seeds = jax.random.split(jax.random.key(seed), 6)
    return {
        "queries": draw_queries(jax.random.fold_in(seeds[5], 71), 0),
        "keys": draw_keys(jax.random.fold_in(seeds[5], 71), 0),
        "values": gaussian(seeds[2], (TOKENS, HEADS * HEAD_DIM), 2.0, 8.0, ((0, 128),)),
        "cotangent": gaussian(seeds[3], (TOKENS, HEADS * HEAD_DIM), 1.0, 6.0, ((0, 128),)),
        "window": draw_window(jax.random.fold_in(seeds[5], 71), 0),
    }


masked_score = -1.0e30


def bround(array):
    return lax.optimization_barrier(array.astype(jnp.bfloat16)).astype(jnp.float32)


def reference(queries, keys, values, cotangent, window):
    factor = HEAD_DIM ** -0.5
    shape_five = (N_GROUP, N_TILE, TILE_TOK, HEADS, HEAD_DIM)
    flat_shape = (FRAME_TOK, HEADS, HEAD_DIM)
    query_all = queries.reshape(shape_five)
    key_all = keys.reshape(shape_five)
    value_all = values.reshape(shape_five)
    cot_all = cotangent.reshape(shape_five)
    front_pad = jnp.zeros((N_TILE, PAST, TILE_TOK, HEADS, HEAD_DIM), jnp.float32)
    key_tiles = jnp.concatenate([front_pad, jnp.transpose(key_all, (1, 0, 2, 3, 4)).astype(jnp.float32)], axis=1)
    value_tiles = jnp.concatenate([front_pad, jnp.transpose(value_all, (1, 0, 2, 3, 4)).astype(jnp.float32)], axis=1)
    places = jnp.arange(FRAME_TOK).astype(jnp.int32)
    spacing = jnp.abs(places[:, None] - places[None, :])
    near_mask = spacing[None, :, :] <= window[:, None, None]
    group_ids = jnp.arange(N_GROUP).astype(jnp.int32)
    lag_ids = jnp.arange(PAST).astype(jnp.int32)

    def per_group(carry, group):
        acc_keys, acc_values = carry
        query_here = query_all[group].astype(jnp.float32)
        key_here = key_all[group].astype(jnp.float32).reshape(flat_shape)
        value_here = value_all[group].astype(jnp.float32).reshape(flat_shape)
        cot_here = cot_all[group].astype(jnp.float32)
        query_flat = query_here.reshape(flat_shape)
        cot_flat = cot_here.reshape(flat_shape)
        window_keys = lax.dynamic_slice_in_dim(key_tiles, group, PAST, 1)
        window_values = lax.dynamic_slice_in_dim(value_tiles, group, PAST, 1)
        near_scores = jnp.einsum('qhd,khd->hqk', query_flat, key_here) * factor
        near_scores = jnp.where(near_mask, near_scores, masked_score)
        past_mask = (group - PAST + lag_ids >= 0)[None, None, None, :, None]
        past_five = jnp.einsum('tqhd,tnkhd->thqnk', query_here, window_keys) * factor
        past_five = jnp.where(past_mask, past_five, masked_score)
        past_scores = jnp.transpose(past_five, (1, 0, 2, 3, 4)).reshape(HEADS, FRAME_TOK, PAST * TILE_TOK)
        top_score = jnp.maximum(near_scores.max(-1), past_scores.max(-1))
        summed = jnp.exp(near_scores - top_score[..., None]).sum(-1) + jnp.exp(past_scores - top_score[..., None]).sum(-1)
        lse = top_score + jnp.log(summed)
        near_probs = jnp.exp(near_scores - lse[..., None])
        past_probs = jnp.exp(past_scores - lse[..., None])
        near_round = bround(near_probs)
        past_round = bround(past_probs).reshape(HEADS, N_TILE, TILE_TOK, PAST, TILE_TOK)
        output = jnp.einsum('hqk,khd->qhd', near_round, value_here).reshape(N_TILE, TILE_TOK, HEADS, HEAD_DIM)
        output = output + jnp.einsum('htqnk,tnkhd->tqhd', past_round, window_values)
        output_b = output.astype(jnp.bfloat16)
        delta = jnp.sum(cot_here * output_b.astype(jnp.float32), -1)
        delta_heads = jnp.transpose(delta, (2, 0, 1)).reshape(HEADS, FRAME_TOK)
        near_dprob = jnp.einsum('qhd,khd->hqk', cot_flat, value_here)
        near_dscore = bround(near_probs * (near_dprob - delta_heads[..., None]))
        past_dprob = jnp.einsum('tqhd,tnkhd->htqnk', cot_here, window_values).reshape(HEADS, FRAME_TOK, PAST * TILE_TOK)
        past_dscore = bround(past_probs * (past_dprob - delta_heads[..., None]))
        past_dfive = past_dscore.reshape(HEADS, N_TILE, TILE_TOK, PAST, TILE_TOK)
        grad_q = jnp.einsum('hqk,khd->qhd', near_dscore, key_here).reshape(N_TILE, TILE_TOK, HEADS, HEAD_DIM)
        grad_q = factor * (grad_q + jnp.einsum('htqnk,tnkhd->tqhd', past_dfive, window_keys))
        near_key = factor * jnp.einsum('hqk,qhd->khd', near_dscore, query_flat)
        near_value = jnp.einsum('hqk,qhd->khd', near_round, cot_flat)
        part_key = bround(factor * jnp.einsum('htqnk,tqhd->tnkhd', past_dfive, query_here))
        part_value = bround(jnp.einsum('htqnk,tqhd->tnkhd', past_round, cot_here))
        acc_keys = lax.dynamic_update_slice_in_dim(acc_keys, lax.dynamic_slice_in_dim(acc_keys, group, PAST, 1) + part_key, group, 1)
        acc_values = lax.dynamic_update_slice_in_dim(acc_values, lax.dynamic_slice_in_dim(acc_values, group, PAST, 1) + part_value, group, 1)
        return (acc_keys, acc_values), (output_b, grad_q.astype(jnp.bfloat16), near_key, near_value)

    zero_acc = jnp.zeros((N_TILE, PAST + N_GROUP, TILE_TOK, HEADS, HEAD_DIM), jnp.float32)
    (acc_keys, acc_values), stacked = lax.scan(per_group, (zero_acc, zero_acc), group_ids)
    outputs, grad_q, near_key, near_value = stacked
    acc_keys = acc_keys[:, PAST:]
    acc_values = acc_values[:, PAST:]
    full_shape = (TOKENS, HEADS * HEAD_DIM)
    grad_k = (near_key.reshape(shape_five) + jnp.transpose(acc_keys, (1, 0, 2, 3, 4))).astype(jnp.bfloat16)
    grad_v = (near_value.reshape(shape_five) + jnp.transpose(acc_values, (1, 0, 2, 3, 4))).astype(jnp.bfloat16)
    return (outputs.reshape(full_shape), grad_q.reshape(full_shape), grad_k.reshape(full_shape), grad_v.reshape(full_shape))
```

```python
import functools

import jax
import jax.numpy as jnp
from jax import lax
from jax.experimental import pallas as pl
from jax.experimental.pallas import tpu as pltpu
from jax.sharding import Mesh, PartitionSpec as P

HEADS = 20
DIM = 128
TOK = 128
HALO = 32
N_Z, N_Y, N_X = 4, 4, 2
N_LOC = N_Y * N_X
FULL = 2
SLOTS = 3
HALF = TOK // 2
Q_ROWS = FULL * TOK + HALF
LOW = -1.0e30
FACTOR = DIM ** -0.5
LOG2E = 1.4426950408889634
AXES = ("z", "y", "xh", "xl", "core")
F32 = jnp.float32
BF16 = jnp.bfloat16


def head_of(place, slot):
    y, x = place // N_X, place % N_X
    return 5 * y + (2 * x + slot if slot < FULL else 4)


def cols(head):
    return slice(head * DIM, (head + 1) * DIM)


def pack_kv_kernel(k_ref, v_ref, out_ref):
    for place in range(N_LOC):
        for slot in range(SLOTS):
            head = head_of(place, slot)
            out_ref[place, 0, slot] = k_ref[:, cols(head)]
            out_ref[place, 1, slot] = v_ref[:, cols(head)]


def pack_q_kernel(q_ref, do_ref, out_ref):
    for place in range(N_LOC):
        start = (place % N_X) * HALF
        for kind, ref in enumerate((q_ref, do_ref)):
            for slot in range(FULL):
                out_ref[place, kind, slot * TOK : (slot + 1) * TOK] = ref[:, cols(head_of(place, slot))]
            out_ref[place, kind, FULL * TOK : Q_ROWS] = ref[start : start + HALF, cols(head_of(place, FULL))]


def unpack_q_kernel(in_ref, o_ref, dq_ref):
    for place in range(N_LOC):
        start = (place % N_X) * HALF
        for kind, ref in enumerate((o_ref, dq_ref)):
            for slot in range(FULL):
                ref[:, cols(head_of(place, slot))] = in_ref[place, kind, slot * TOK : (slot + 1) * TOK]
            ref[start : start + HALF, cols(head_of(place, FULL))] = in_ref[place, kind, FULL * TOK : Q_ROWS]


def unpack_kv_kernel(in_ref, dk_ref, dv_ref):
    for y in range(N_Y):
        for kind, ref in enumerate((dk_ref, dv_ref)):
            for x in range(N_X):
                place = y * N_X + x
                for slot in range(FULL):
                    ref[:, cols(head_of(place, slot))] = in_ref[place, kind, slot]
            both = in_ref[y * N_X, kind, FULL].astype(F32) + in_ref[y * N_X + 1, kind, FULL].astype(F32)
            ref[:, cols(head_of(y * N_X, FULL))] = both.astype(BF16)


def merge_kernel(own_ref, past_ref, from_low_ref, from_high_ref, out_ref):
    for loc in range(N_LOC):
        for kind in range(2):
            total = own_ref[loc, kind, 0] + past_ref[loc, kind, 0].astype(F32)
            first = total[:HALO] + from_low_ref[loc, kind, 0].astype(F32)
            last = total[TOK - HALO :] + from_high_ref[loc, kind, 0].astype(F32)
            out_ref[loc, kind, 0, :HALO] = first.astype(BF16)
            out_ref[loc, kind, 0, HALO : TOK - HALO] = total[HALO : TOK - HALO].astype(BF16)
            out_ref[loc, kind, 0, TOK - HALO :] = last.astype(BF16)


def dot_nt(a, b):
    return lax.dot_general(a, b, (((1,), (1,)), ((), ())), preferred_element_type=F32)


def dot_nn(a, b):
    return lax.dot_general(a, b, (((1,), (0,)), ((), ())), preferred_element_type=F32)


N_WIN = 10
WIN = N_WIN * TOK
ROWS = WIN + TOK


def attention_job(
    rows, row_start, pair, slot, window, z, xh, tile,
    q_ref, low_ref, high_ref, o_ref, dlow_ref, dhigh_ref,
    kcat, vcat, ktr, vtr, dkacc, dvacc, s_ref, p_ref, ds_ref,
):
    lanes = 2 * rows
    base = pl.multiple_of(pair * (2 * TOK), 2 * TOK)
    la, lb = 2 * pair, 2 * pair + 1
    q = jnp.concatenate([q_ref[la, 0, row_start : row_start + rows], q_ref[lb, 0, row_start : row_start + rows]], axis=0)
    do = jnp.concatenate([q_ref[la, 1, row_start : row_start + rows], q_ref[lb, 1, row_start : row_start + rows]], axis=0)

    def border(kind):
        return jnp.concatenate([low_ref[la, kind, 0], high_ref[la, kind, 0], low_ref[lb, kind, 0], high_ref[lb, kind, 0]], axis=0)

    k_border, v_border = border(0), border(1)
    scale = FACTOR * LOG2E
    row = lax.broadcasted_iota(jnp.int32, (TOK, lanes), 0)
    lane = lax.broadcasted_iota(jnp.int32, (TOK, lanes), 1)
    is_b = lane >= rows
    place = jnp.where(is_b, lane - rows, lane) + (xh * HALF if rows < TOK else 0)
    near = jnp.abs(place - row) <= window
    half_row = row % (2 * HALO)
    border_place = jnp.where(half_row < HALO, half_row - HALO, half_row + TOK - HALO)
    first = jnp.where(tile > 0, -HALO, 0)
    end = jnp.where(tile < 3, TOK + HALO, TOK)
    border_ok = (jnp.abs(place - border_place) <= window) & (border_place >= first) & (border_place < end)
    border_ok &= jnp.where(row >= 2 * HALO, 1, 0) == jnp.where(is_b, 1, 0)

    tops = []
    biases = []
    for b in range(N_WIN + 1):
        if b < N_WIN:
            keys = kcat[pl.ds(base + b * TOK, TOK), :]
        else:
            keys = k_border
        s = dot_nt(keys, q)
        if b == 0:
            s = jnp.where(is_b, LOW, s)
        elif b == 8:
            s = jnp.where(is_b | near, s, LOW)
        elif b == 9:
            s = jnp.where(is_b & near, s, LOW)
        elif b == N_WIN:
            s = jnp.where(border_ok, s, LOW)
        s_ref[b * TOK : (b + 1) * TOK, :lanes] = s
        top = jnp.max(s.reshape(TOK // 8, 8, lanes), axis=0) * scale
        if b < 8:
            bias = jnp.where((z == 0) & (2 * pair + b < N_LOC), LOW, 0.0)
            top = top + bias
        else:
            bias = None
        tops.append(top)
        biases.append(bias)
    top = functools.reduce(jnp.maximum, tops)
    top = jnp.max(top, axis=0, keepdims=True)
    total = jnp.zeros((8, lanes), F32)
    for b in range(N_WIN + 1):
        shift = -top if biases[b] is None else biases[b] - top
        e = jnp.exp2(s_ref[b * TOK : (b + 1) * TOK, :lanes] * scale + shift)
        s_ref[b * TOK : (b + 1) * TOK, :lanes] = e
        total = total + jnp.sum(e.reshape(TOK // 8, 8, lanes), axis=0)
    inverse = 1.0 / jnp.sum(total, axis=0, keepdims=True)
    for b in range(N_WIN + 1):
        probs = s_ref[b * TOK : (b + 1) * TOK, :lanes] * inverse
        s_ref[b * TOK : (b + 1) * TOK, :lanes] = probs
        p_ref[b * TOK : (b + 1) * TOK, :lanes] = probs.astype(BF16)
    out_t = dot_nn(vtr[:, pl.ds(base, WIN)], p_ref[:WIN, :lanes])
    out_t = out_t + dot_nn(v_border.T, p_ref[WIN:, :lanes])
    out_b = out_t.astype(BF16).astype(F32)
    delta = jnp.sum(out_b * do.astype(F32).T, axis=0, keepdims=True)
    out = out_b.T.astype(BF16)
    o_ref[la, 0, row_start : row_start + rows] = out[:rows]
    o_ref[lb, 0, row_start : row_start + rows] = out[rows:]
    for b in range(N_WIN + 1):
        if b < N_WIN:
            vals = vcat[pl.ds(base + b * TOK, TOK), :]
        else:
            vals = v_border
        dp = dot_nt(vals, do)
        ds = s_ref[b * TOK : (b + 1) * TOK, :lanes] * (dp - delta)
        ds_ref[b * TOK : (b + 1) * TOK, :lanes] = ds.astype(BF16)
    dq_t = dot_nn(ktr[:, pl.ds(base, WIN)], ds_ref[:WIN, :lanes])
    dq_t = dq_t + dot_nn(k_border.T, ds_ref[WIN:, :lanes])
    dq = (dq_t * FACTOR).T.astype(BF16)
    o_ref[la, 1, row_start : row_start + rows] = dq[:rows]
    o_ref[lb, 1, row_start : row_start + rows] = dq[rows:]
    for b in range(N_WIN):
        at = pl.ds(base + b * TOK, TOK)
        dvacc[at, :] += dot_nn(p_ref[b * TOK : (b + 1) * TOK, :lanes], do)
        dkacc[at, :] += dot_nn(ds_ref[b * TOK : (b + 1) * TOK, :lanes], q)
    dv_border = dot_nn(p_ref[WIN:, :lanes], do).astype(BF16)
    dk_border = (dot_nn(ds_ref[WIN:, :lanes], q) * FACTOR).astype(BF16)
    for kind, grad in enumerate((dk_border, dv_border)):
        for which, loc in enumerate((la, lb)):
            at = which * 2 * HALO
            dlow_ref[loc, kind, 0] = grad[at : at + HALO]
            dhigh_ref[loc, kind, 0] = grad[at + HALO : at + 2 * HALO]


def attention_kernel(
    window_ref, kv_ref, past_ref, low_ref, high_ref, q_ref,
    o_ref, own_ref, back_ref, dlow_ref, dhigh_ref,
    kcat, vcat, ktr, vtr, dkacc, dvacc, s_ref, p_ref, ds_ref,
):
    slot, pair = pl.program_id(0), pl.program_id(1)
    z, y, xh = lax.axis_index("z"), lax.axis_index("y"), lax.axis_index("xh")
    tile = lax.axis_index("xl") * 2 + lax.axis_index("core")

    @pl.when(pair == 0)
    def _():
        for kind, cat, tr in ((0, kcat, ktr), (1, vcat, vtr)):
            for loc in range(2 * N_LOC):
                src = past_ref if loc < N_LOC else kv_ref
                block = src[loc % N_LOC, kind, 0]
                cat[loc * TOK : (loc + 1) * TOK, :] = block
                tr[:, loc * TOK : (loc + 1) * TOK] = block.T
        dkacc[...] = jnp.zeros_like(dkacc)
        dvacc[...] = jnp.zeros_like(dvacc)

    head = 5 * y + jnp.where(slot < FULL, 2 * xh + slot, 4)
    window = window_ref[head]
    rest = (
        q_ref, low_ref, high_ref, o_ref, dlow_ref, dhigh_ref,
        kcat, vcat, ktr, vtr, dkacc, dvacc, s_ref, p_ref, ds_ref,
    )
    for which in range(SLOTS):
        @pl.when(slot == which)
        def _(which=which):
            rows = TOK if which < FULL else HALF
            attention_job(rows, which * TOK, pair, slot, window, z, xh, tile, *rest)

    @pl.when(pair == N_LOC // 2 - 1)
    def _():
        for kind, acc in ((0, dkacc), (1, dvacc)):
            for loc in range(N_LOC):
                low = acc[loc * TOK : (loc + 1) * TOK, :]
                high = acc[(N_LOC + loc) * TOK : (N_LOC + loc + 1) * TOK, :]
                back_ref[loc, kind, 0] = (low * FACTOR if kind == 0 else low).astype(BF16)
                own_ref[loc, kind, 0] = high * FACTOR if kind == 0 else high


def whole(shape):
    return pl.BlockSpec(shape, lambda *_: (0,) * len(shape))


def simple_call(kernel, out_shapes, *args):
    outs = [jax.ShapeDtypeStruct(s, BF16) for s in out_shapes]
    moved = sum(a.size * a.dtype.itemsize for a in args) + sum(2 * o.size for o in outs)
    return pl.pallas_call(
        kernel,
        grid=(1,),
        out_shape=outs,
        in_specs=[whole(a.shape) for a in args],
        out_specs=[whole(s) for s in out_shapes],
        compiler_params=pltpu.CompilerParams(vmem_limit_bytes=32 * 2**20),
        cost_estimate=pl.CostEstimate(flops=0, bytes_accessed=moved, transcendentals=0),
    )(*args)


def by_slot(rows):
    return pl.BlockSpec((N_LOC, 2, 1, rows, DIM), lambda slot, *_: (0, 0, slot, 0, 0))


def attention(window, kv, past, low, high, qdo):
    kv_shape = (N_LOC, 2, SLOTS, TOK, DIM)
    border_shape = (N_LOC, 2, SLOTS, HALO, DIM)
    return pl.pallas_call(
        attention_kernel,
        grid=(SLOTS, N_LOC // 2),
        out_shape=[
            jax.ShapeDtypeStruct(qdo.shape, BF16),
            jax.ShapeDtypeStruct(kv_shape, F32),
            jax.ShapeDtypeStruct(kv_shape, BF16),
            jax.ShapeDtypeStruct(border_shape, BF16),
            jax.ShapeDtypeStruct(border_shape, BF16),
        ],
        in_specs=[
            pl.BlockSpec(memory_space=pltpu.SMEM),
            by_slot(TOK), by_slot(TOK), by_slot(HALO), by_slot(HALO),
            whole(qdo.shape),
        ],
        out_specs=[whole(qdo.shape), by_slot(TOK), by_slot(TOK), by_slot(HALO), by_slot(HALO)],
        scratch_shapes=[
            pltpu.VMEM((2 * N_LOC * TOK, DIM), BF16),
            pltpu.VMEM((2 * N_LOC * TOK, DIM), BF16),
            pltpu.VMEM((DIM, 2 * N_LOC * TOK), BF16),
            pltpu.VMEM((DIM, 2 * N_LOC * TOK), BF16),
            pltpu.VMEM((2 * N_LOC * TOK, DIM), F32),
            pltpu.VMEM((2 * N_LOC * TOK, DIM), F32),
            pltpu.VMEM((ROWS, 2 * TOK), F32),
            pltpu.VMEM((ROWS, 2 * TOK), BF16),
            pltpu.VMEM((ROWS, 2 * TOK), BF16),
        ],
        compiler_params=pltpu.CompilerParams(vmem_limit_bytes=48 * 2**20),
        cost_estimate=pl.CostEstimate(flops=6 * 10**9, bytes_accessed=10**7, transcendentals=4 * 10**6),
    )(window, kv, past, low, high, qdo)


def swap(x):
    return lax.all_to_all(x, ("y", "xh"), 0, 0)


def shards(queries, keys, values, cotangent, window):
    kv_shape = (N_LOC, 2, SLOTS, TOK, DIM)
    q_shape = (N_LOC, 2, Q_ROWS, DIM)
    up = [(i, i + 1) for i in range(N_Z - 1)]
    down = [(i + 1, i) for i in range(N_Z - 1)]
    tiles = ("xl", "core")
    (packed_kv,) = simple_call(pack_kv_kernel, [kv_shape], keys, values)
    (packed_q,) = simple_call(pack_q_kernel, [q_shape], queries, cotangent)
    kv = swap(packed_kv)
    past = lax.ppermute(kv, "z", up)
    low = lax.ppermute(kv[:, :, :, TOK - HALO :], tiles, up)
    high = lax.ppermute(kv[:, :, :, :HALO], tiles, down)
    qdo = swap(packed_q)
    odq, own, back, dlow, dhigh = attention(window, kv, past, low, high, qdo)
    past_grads = lax.ppermute(back, "z", down)
    from_high = lax.ppermute(dlow, tiles, down)
    from_low = lax.ppermute(dhigh, tiles, up)
    out_q = swap(odq)
    (merged,) = pl.pallas_call(
        merge_kernel,
        grid=(SLOTS,),
        out_shape=[jax.ShapeDtypeStruct(kv_shape, BF16)],
        in_specs=[by_slot(TOK), by_slot(TOK), by_slot(HALO), by_slot(HALO)],
        out_specs=[by_slot(TOK)],
        compiler_params=pltpu.CompilerParams(vmem_limit_bytes=32 * 2**20),
        cost_estimate=pl.CostEstimate(flops=10**6, bytes_accessed=8 * 10**6, transcendentals=0),
    )(own, past_grads, from_low, from_high)
    out_kv = swap(merged)
    attended, grad_queries = simple_call(unpack_q_kernel, [queries.shape] * 2, out_q)
    grad_keys, grad_values = simple_call(unpack_kv_kernel, [keys.shape] * 2, out_kv)
    return attended, grad_queries, grad_keys, grad_values


def solution(mesh):
    fine = Mesh(mesh.devices.reshape(N_Z, N_Y, N_X, 2, 2), AXES)
    rows = P(AXES, None)
    return jax.shard_map(
        shards,
        mesh=fine,
        in_specs=(rows, rows, rows, rows, P()),
        out_specs=(rows, rows, rows, rows),
        check_vma=False,
    )
```

```python
import functools
import math

import jax
import jax.numpy as jnp
from jax import lax
from jax.experimental import pallas as pl
from jax.experimental.pallas import tpu as pltpu
from jax.sharding import Mesh, PartitionSpec as P

HEADS = 20
DIM = 128
TOK = 128
HALO = 32
N_Z, N_Y, N_X = 4, 4, 2
N_LOC = N_Y * N_X
FULL = 2
SLOTS = 3
HALF = TOK // 2
Q_ROWS = FULL * TOK + HALF
LOW = -1.0e30
FACTOR = DIM ** -0.5
LOG2E = 1.4426950408889634
ATTEND_MIB = 60
AXES = ("z", "y", "xh", "xl", "core")
PLACES = ("y", "xh")
TILES = ("xl", "core")
F32 = jnp.float32
BF16 = jnp.bfloat16


def head_cols(place, slot):
    head = place // N_X * 5 + (place % N_X * 2 + slot if slot < FULL else 4)
    return slice(head * DIM, (head + 1) * DIM)


def pack_keys_kernel(k_ref, v_ref, kv_ref):
    for place in range(N_LOC):
        for kind, ref in enumerate((k_ref, v_ref)):
            for slot in range(SLOTS):
                kv_ref[place, kind, slot] = ref[:, head_cols(place, slot)]


def pack_queries_kernel(q_ref, do_ref, qdo_ref):
    for place in range(N_LOC):
        start = place % N_X * HALF
        for kind, ref in enumerate((q_ref, do_ref)):
            for slot in range(FULL):
                qdo_ref[place, kind, slot * TOK : (slot + 1) * TOK] = ref[:, head_cols(place, slot)]
            qdo_ref[place, kind, FULL * TOK :] = ref[start : start + HALF, head_cols(place, FULL)]


def unpack_queries_kernel(odq_ref, o_ref, dq_ref):
    for place in range(N_LOC):
        start = place % N_X * HALF
        for kind, ref in enumerate((o_ref, dq_ref)):
            for slot in range(FULL):
                ref[:, head_cols(place, slot)] = odq_ref[place, kind, slot * TOK : (slot + 1) * TOK]
            ref[start : start + HALF, head_cols(place, FULL)] = odq_ref[place, kind, FULL * TOK :]


def unpack_keys_kernel(grads_ref, dk_ref, dv_ref):
    for kind, ref in enumerate((dk_ref, dv_ref)):
        for place in range(N_LOC):
            for slot in range(FULL):
                ref[:, head_cols(place, slot)] = grads_ref[place, kind, slot]
        for place in range(0, N_LOC, N_X):
            both = grads_ref[place, kind, FULL].astype(F32) + grads_ref[place + 1, kind, FULL].astype(F32)
            ref[:, head_cols(place, FULL)] = both.astype(BF16)


def merge_kernel(own_ref, got_ref, from_low_ref, from_high_ref, out_ref):
    for loc in range(own_ref.shape[0]):
        for kind in range(2):
            for slot in range(SLOTS):
                at = (loc, kind, slot)
                total = own_ref[at].astype(F32) + got_ref[at].astype(F32)
                first = total[:HALO] + from_low_ref[at].astype(F32)
                last = total[TOK - HALO :] + from_high_ref[at].astype(F32)
                out_ref[loc, kind, slot, :HALO] = first.astype(BF16)
                out_ref[loc, kind, slot, HALO : TOK - HALO] = total[HALO : TOK - HALO].astype(BF16)
                out_ref[loc, kind, slot, TOK - HALO :] = last.astype(BF16)


def dot_nt(a, b):
    return lax.dot_general(a, b, (((1,), (1,)), ((), ())), preferred_element_type=F32)


def dot_nn(a, b):
    return lax.dot_general(a, b, (((1,), (0,)), ((), ())), preferred_element_type=F32)


LANES = 2 * TOK
UNIT = 2 * TOK
CAT = 2 * N_LOC * TOK
N_PAST = 8


def queries_job(
    rows, job, window, no_past, xh, tile, get_query, get_border, put_query, put_border,
    kcat, vcat, ktr, vtr, q_all, do_all, s_ref, p_ref, ds_ref,
):
    groups = LANES // rows
    n_win = N_PAST + groups
    n_blocks = n_win + groups // 2
    win = n_win * TOK
    base = job * groups * TOK
    locs = [job * groups + g for g in range(groups)]
    lanes = slice(job * LANES, (job + 1) * LANES)
    scale = FACTOR * LOG2E
    window_rows = slice(base, base + win)
    q = jnp.concatenate([get_query(loc, 0) for loc in locs], axis=0)
    do = jnp.concatenate([get_query(loc, 1) for loc in locs], axis=0)
    q_all[lanes, :] = q

    def border(kind, half):
        parts = [get_border(loc, kind, side) for loc in locs[2 * half : 2 * half + 2] for side in range(2)]
        return jnp.concatenate(parts, axis=0)

    row = lax.broadcasted_iota(jnp.int32, (TOK, LANES), 0)
    lane = lax.broadcasted_iota(jnp.int32, (TOK, LANES), 1)
    group = lane // rows
    place = lane - group * rows + (xh * HALF if rows < TOK else 0)
    near = jnp.abs(place - row) <= window
    half_row = row % (2 * HALO)
    border_place = jnp.where(half_row < HALO, half_row - HALO, half_row + TOK - HALO)
    first = jnp.where(tile > 0, -HALO, 0)
    end = jnp.where(tile < 3, TOK + HALO, TOK)
    border_near = (jnp.abs(place - border_place) <= window) & (border_place >= first) & (border_place < end)
    row_group = row // (2 * HALO)

    k_borders = [border(0, half) for half in range(groups // 2)]
    v_borders = [border(1, half) for half in range(groups // 2)]
    top = None
    biases = []
    for b in range(n_blocks):
        keys = kcat[base + b * TOK : base + (b + 1) * TOK, :] if b < n_win else k_borders[b - n_win]
        s = dot_nt(keys, q)
        if b < groups - 1:
            s = jnp.where(group <= b, s, LOW)
        elif N_PAST <= b < n_win:
            s = jnp.where((group > b - N_PAST) | ((group == b - N_PAST) & near), s, LOW)
        elif b >= n_win:
            s = jnp.where(border_near & (row_group + 2 * (b - n_win) == group), s, LOW)
        s_ref[b * TOK : (b + 1) * TOK, :] = s
        here = jnp.max(s.reshape(TOK // 8, 8, LANES), axis=0) * scale
        bias = None
        if b < N_PAST and job * groups + b < N_LOC:
            bias = jnp.where(no_past, LOW, 0.0)
            here = here + bias
        top = here if top is None else jnp.maximum(top, here)
        biases.append(bias)
    top = jnp.max(top, axis=0, keepdims=True)
    total = jnp.zeros((8, LANES), F32)
    for b in range(n_blocks):
        shift = -top if biases[b] is None else biases[b] - top
        e = jnp.exp2(s_ref[b * TOK : (b + 1) * TOK, :] * scale + shift)
        total = total + jnp.sum(e.reshape(TOK // 8, 8, LANES), axis=0)
        if b < n_win:
            p_ref[base + b * TOK : base + (b + 1) * TOK, lanes] = e.astype(BF16)
        else:
            p_ref[CAT + (b - n_win) * TOK : CAT + (b - n_win + 1) * TOK, lanes] = e.astype(BF16)
    inverse = 1.0 / jnp.sum(total, axis=0, keepdims=True)
    do_t = (do.astype(F32).T * inverse).astype(BF16).astype(F32)
    do = do_t.T.astype(BF16)
    do_all[lanes, :] = do
    out_t = dot_nn(vtr[:, window_rows], p_ref[window_rows, lanes])
    for half in range(groups // 2):
        out_t = out_t + dot_nn(v_borders[half].T, p_ref[CAT + half * TOK : CAT + (half + 1) * TOK, lanes])
    out_b = (out_t * inverse).astype(BF16).astype(F32)
    delta = jnp.sum(out_b * do_t, axis=0, keepdims=True)
    out = out_b.T.astype(BF16)
    for g, loc in enumerate(locs):
        put_query(loc, 0, out[g * rows : (g + 1) * rows])
    for b in range(n_blocks):
        vals = vcat[base + b * TOK : base + (b + 1) * TOK, :] if b < n_win else v_borders[b - n_win]
        at = base + b * TOK if b < n_win else CAT + (b - n_win) * TOK
        ds = p_ref[at : at + TOK, lanes].astype(F32) * (dot_nt(vals, do) - delta)
        ds_ref[at : at + TOK, lanes] = ds.astype(BF16)
    dq_t = dot_nn(ktr[:, window_rows], ds_ref[window_rows, lanes])
    for half in range(groups // 2):
        dq_t = dq_t + dot_nn(k_borders[half].T, ds_ref[CAT + half * TOK : CAT + (half + 1) * TOK, lanes])
    dq = (dq_t * FACTOR).T.astype(BF16)
    for g, loc in enumerate(locs):
        put_query(loc, 1, dq[g * rows : (g + 1) * rows])
    for half in range(groups // 2):
        rows_at = slice(CAT + half * TOK, CAT + (half + 1) * TOK)
        dv_border = dot_nn(p_ref[rows_at, lanes], do).astype(BF16)
        dk_border = (dot_nn(ds_ref[rows_at, lanes], q) * FACTOR).astype(BF16)
        for kind, grad in enumerate((dk_border, dv_border)):
            for which, loc in enumerate(locs[2 * half : 2 * half + 2]):
                at = which * 2 * HALO
                put_border(loc, kind, grad[at : at + HALO], grad[at + HALO : at + 2 * HALO])


def keys_job(rows, put_past, put_own, q_all, do_all, p_ref, ds_ref):
    groups = LANES // rows
    jobs = N_LOC // groups
    for unit in range(CAT // UNIT):
        mine = [j for j in range(jobs) if j * groups // 2 <= unit < j * groups // 2 + (N_PAST + groups) // 2]
        lanes = slice(mine[0] * LANES, (mine[-1] + 1) * LANES)
        at = slice(unit * UNIT, (unit + 1) * UNIT)
        dk = dot_nn(ds_ref[at, lanes], q_all[lanes, :]) * FACTOR
        dv = dot_nn(p_ref[at, lanes], do_all[lanes, :])
        for kind, grad in enumerate((dk, dv)):
            for which in range(2):
                loc = unit * 2 + which
                part = grad[which * TOK : (which + 1) * TOK]
                if loc < N_LOC:
                    put_past(loc, kind, part.astype(BF16))
                else:
                    put_own(loc - N_LOC, kind, part.astype(BF16))


def load_keys(get_past, get_own, kcat, vcat, ktr, vtr):
    for kind, cat, tr in ((0, kcat, ktr), (1, vcat, vtr)):
        for loc in range(2 * N_LOC):
            block = get_past(loc, kind) if loc < N_LOC else get_own(loc - N_LOC, kind)
            cat[loc * TOK : (loc + 1) * TOK, :] = block
            tr[:, loc * TOK : (loc + 1) * TOK] = block.T


def attention_body(rows, window, no_past, get_past, get_own, get_query, get_border, put_query, put_border, put_past, put_own, *scratch):
    kcat, vcat, ktr, vtr, q_all, do_all, s0_ref, s1_ref, p_ref, ds_ref = scratch
    xh, tile = lax.axis_index("xh"), lax.axis_index("xl") * 2 + lax.axis_index("core")
    load_keys(get_past, get_own, kcat, vcat, ktr, vtr)
    for job in range(N_LOC * rows // LANES):
        queries_job(
            rows, job, window, no_past, xh, tile, get_query, get_border, put_query, put_border,
            kcat, vcat, ktr, vtr, q_all, do_all, s1_ref if job % 2 else s0_ref, p_ref, ds_ref,
        )
    keys_job(rows, put_past, put_own, q_all, do_all, p_ref, ds_ref)


def put_into(ref, *rest):
    def put(loc, kind, value):
        ref[(loc, kind, *rest)] = value

    return put


def attention_kernel(
    window_ref, kv_ref, past_ref, low_ref, high_ref, q_ref, o_ref, own_ref, back_ref, dlow_ref, dhigh_ref, *scratch
):
    y, xh = lax.axis_index("y"), lax.axis_index("xh")

    def put_border(loc, kind, low, high):
        dlow_ref[loc, kind, 0] = low
        dhigh_ref[loc, kind, 0] = high

    def slot_work(slot):
        rows = TOK if slot < FULL else HALF
        q_rows = slice(slot * TOK, slot * TOK + rows)

        def put_query(loc, kind, value):
            o_ref[loc, kind, q_rows] = value

        attention_body(
            rows, window_ref[5 * y + (2 * xh + slot if slot < FULL else 4)], lax.axis_index("z") == 0,
            lambda loc, kind: past_ref[loc, kind, 0],
            lambda loc, kind: kv_ref[loc, kind, 0],
            lambda loc, kind: q_ref[loc, kind, q_rows],
            lambda loc, kind, side: (high_ref if side else low_ref)[loc, kind, 0],
            put_query, put_border, put_into(back_ref, 0), put_into(own_ref, 0),
            *scratch,
        )

    for slot in range(SLOTS):
        pl.when(pl.program_id(0) == slot)(functools.partial(slot_work, slot))


SCRATCH = [
    pltpu.VMEM((CAT, DIM), BF16),
    pltpu.VMEM((CAT, DIM), BF16),
    pltpu.VMEM((DIM, CAT), BF16),
    pltpu.VMEM((DIM, CAT), BF16),
    pltpu.VMEM((N_LOC * TOK, DIM), BF16),
    pltpu.VMEM((N_LOC * TOK, DIM), BF16),
    pltpu.VMEM((14 * TOK, LANES), F32),
    pltpu.VMEM((14 * TOK, LANES), F32),
    pltpu.VMEM((CAT + UNIT, N_LOC * TOK), BF16),
    pltpu.VMEM((CAT + UNIT, N_LOC * TOK), BF16),
]
SMEM = pl.BlockSpec(memory_space=pltpu.SMEM)
ANYWHERE = pl.BlockSpec(memory_space=pl.ANY)
KV_SHAPE = (N_LOC, 2, SLOTS, TOK, DIM)
BORDER_SHAPE = (N_LOC, 2, SLOTS, HALO, DIM)
Q_SHAPE = (N_LOC, 2, Q_ROWS, DIM)


def call(kernel, grid, in_specs, args, outs, flops=0, scratch=(), limit=60):
    moved = sum(a.size * a.dtype.itemsize for a in args) + sum(2 * math.prod(shape) for shape, _ in outs)
    return pl.pallas_call(
        kernel,
        grid=(grid,),
        out_shape=[jax.ShapeDtypeStruct(shape, BF16) for shape, _ in outs],
        in_specs=in_specs,
        out_specs=[spec for _, spec in outs],
        scratch_shapes=list(scratch),
        compiler_params=pltpu.CompilerParams(vmem_limit_bytes=limit * 2**20),
        cost_estimate=pl.CostEstimate(flops=flops, bytes_accessed=moved, transcendentals=0),
    )(*args)


def simple(kernel, args, outs, limit=32):
    return call(kernel, 1, [whole(a.shape) for a in args], args, [(o, whole(o)) for o in outs], limit=limit)


def by_slot(rows):
    return pl.BlockSpec((N_LOC, 2, 1, rows, DIM), lambda slot: (0, 0, slot, 0, 0))


def whole(shape):
    return pl.BlockSpec(shape, lambda _: (0,) * len(shape))


def split(shape, parts):
    return pl.BlockSpec((shape[0] // parts, *shape[1:]), lambda i: (i, *[0] * (len(shape) - 1)))


def attend(window, kv, past, low, high, qdo):
    specs = [SMEM, by_slot(TOK), by_slot(TOK), by_slot(HALO), by_slot(HALO), whole(Q_SHAPE)]
    outs = [(Q_SHAPE, whole(Q_SHAPE))] + [(KV_SHAPE, by_slot(TOK))] * 2 + [(BORDER_SHAPE, by_slot(HALO))] * 2
    return call(attention_kernel, SLOTS, specs, (window, kv, past, low, high, qdo), outs, 10**10, SCRATCH, limit=ATTEND_MIB)


def exchange(x):
    return lax.all_to_all(x, PLACES, 0, 0)


def shards(queries, keys, values, cotangent, window):
    up = [(i, i + 1) for i in range(N_Z - 1)]
    down = [(i + 1, i) for i in range(N_Z - 1)]
    (packed_kv,) = simple(pack_keys_kernel, (keys, values), [KV_SHAPE])
    (packed_q,) = simple(pack_queries_kernel, (queries, cotangent), [Q_SHAPE])
    kv = exchange(packed_kv)
    past = lax.ppermute(kv, "z", up)
    low = lax.ppermute(kv[:, :, :, TOK - HALO :], TILES, up)
    high = lax.ppermute(kv[:, :, :, :HALO], TILES, down)
    qdo = exchange(packed_q)
    odq, own, back, dlow, dhigh = attend(window, kv, past, low, high, qdo)
    got = lax.ppermute(back, "z", down)
    from_high = lax.ppermute(dlow, TILES, down)
    from_low = lax.ppermute(dhigh, TILES, up)
    out_q = exchange(odq)
    args = (own, got, from_low, from_high)
    outs = [(KV_SHAPE, split(KV_SHAPE, 4))]
    (merged,) = call(merge_kernel, 4, [split(a.shape, 4) for a in args], args, outs, limit=32)
    out_kv = exchange(merged)
    attended, grad_queries = simple(unpack_queries_kernel, (out_q,), [queries.shape] * 2)
    grad_keys, grad_values = simple(unpack_keys_kernel, (out_kv,), [keys.shape] * 2)
    return attended, grad_queries, grad_keys, grad_values


def solution(mesh):
    fine = Mesh(mesh.devices.reshape(N_Z, N_Y, N_X, 2, 2), AXES)
    rows = P(AXES, None)
    return jax.shard_map(
        shards,
        mesh=fine,
        in_specs=(rows, rows, rows, rows, P()),
        out_specs=(rows, rows, rows, rows),
        check_vma=False,
    )
```

```python
import functools
import math

import jax
import jax.numpy as jnp
from jax import lax
from jax.experimental import pallas as pl
from jax.experimental.pallas import tpu as pltpu
from jax.sharding import Mesh, PartitionSpec as P

HEADS = 20
DIM = 128
TOK = 128
HALO = 32
N_Z, N_Y, N_X = 4, 4, 2
N_LOC = N_Y * N_X
FULL = 2
SLOTS = 3
HALF = TOK // 2
Q_ROWS = FULL * TOK + HALF
ALL_ROWS = Q_ROWS + TOK
LOW = -1.0e30
FACTOR = DIM ** -0.5
LOG2E = 1.4426950408889634
ATTEND_MIB = 60
AXES = ("z", "y", "xh", "xl", "core")
PLACES = ("y", "xh")
TILES = ("xl", "core")
F32 = jnp.float32
BF16 = jnp.bfloat16


def head_cols(place, slot):
    head = place // N_X * 5 + (place % N_X * 2 + slot if slot < FULL else 4)
    return slice(head * DIM, (head + 1) * DIM)


def pack_keys_kernel(k_ref, v_ref, kv_ref, raw_ref):
    for y in range(N_Y):
        raw_ref[y, 0] = k_ref[:, head_cols(y * N_X, FULL)]
        raw_ref[y, 1] = v_ref[:, head_cols(y * N_X, FULL)]
    for place in range(N_LOC):
        for kind, ref in enumerate((k_ref, v_ref)):
            for slot in range(SLOTS):
                kv_ref[place, kind, slot] = ref[:, head_cols(place, slot)]


def pack_queries_kernel(q_ref, do_ref, raw_ref, qdo_ref):
    for place in range(N_LOC):
        start = place % N_X * HALF
        for kind, ref in enumerate((q_ref, do_ref)):
            for slot in range(FULL):
                qdo_ref[place, kind, slot * TOK : (slot + 1) * TOK] = ref[:, head_cols(place, slot)]
            qdo_ref[place, kind, FULL * TOK : Q_ROWS] = ref[start : start + HALF, head_cols(place, FULL)]
            qdo_ref[place, kind, Q_ROWS:] = raw_ref[place // N_X, kind]


def unpack_queries_kernel(odq_ref, o_ref, dq_ref, raw_ref):
    for place in range(N_LOC):
        start = place % N_X * HALF
        for kind, ref in enumerate((o_ref, dq_ref)):
            for slot in range(FULL):
                ref[:, head_cols(place, slot)] = odq_ref[place, kind, slot * TOK : (slot + 1) * TOK]
            ref[start : start + HALF, head_cols(place, FULL)] = odq_ref[place, kind, FULL * TOK : Q_ROWS]
    for kind in range(2):
        for y in range(N_Y):
            first, second = odq_ref[y * N_X, kind, Q_ROWS:], odq_ref[y * N_X + 1, kind, Q_ROWS:]
            raw_ref[y, kind] = (first.astype(F32) + second.astype(F32)).astype(BF16)


def unpack_keys_kernel(grads_ref, raw_ref, dk_ref, dv_ref):
    for kind, ref in enumerate((dk_ref, dv_ref)):
        for place in range(N_LOC):
            for slot in range(FULL):
                ref[:, head_cols(place, slot)] = grads_ref[place, kind, slot]
        for place in range(0, N_LOC, N_X):
            both = grads_ref[place, kind, FULL].astype(F32) + grads_ref[place + 1, kind, FULL].astype(F32)
            both = both + raw_ref[place // N_X, kind].astype(F32)
            ref[:, head_cols(place, FULL)] = both.astype(BF16)


def merge_kernel(own_ref, got_ref, from_low_ref, from_high_ref, out_ref):
    for loc in range(own_ref.shape[0]):
        for kind in range(2):
            for slot in range(SLOTS):
                at = (loc, kind, slot)
                total = own_ref[at].astype(F32)
                if slot < FULL:
                    total = total + got_ref[at].astype(F32)
                first = total[:HALO] + from_low_ref[at].astype(F32)
                last = total[TOK - HALO :] + from_high_ref[at].astype(F32)
                out_ref[loc, kind, slot, :HALO] = first.astype(BF16)
                out_ref[loc, kind, slot, HALO : TOK - HALO] = total[HALO : TOK - HALO].astype(BF16)
                out_ref[loc, kind, slot, TOK - HALO :] = last.astype(BF16)


def dot_nt(a, b):
    return lax.dot_general(a, b, (((1,), (1,)), ((), ())), preferred_element_type=F32)


def dot_nn(a, b):
    return lax.dot_general(a, b, (((1,), (0,)), ((), ())), preferred_element_type=F32)


LANES = 2 * TOK
UNIT = 2 * TOK
CAT = 2 * N_LOC * TOK
N_PAST = 8


def queries_job(
    rows, job, window, no_past, xh, tile, get_query, get_border, put_query, put_border,
    kcat, vcat, ktr, vtr, q_all, do_all, s_ref, p_ref, ds_ref,
):
    groups = LANES // rows
    n_win = N_PAST + groups
    n_blocks = n_win + groups // 2
    win = n_win * TOK
    base = job * groups * TOK
    locs = [job * groups + g for g in range(groups)]
    lanes = slice(job * LANES, (job + 1) * LANES)
    scale = FACTOR * LOG2E
    window_rows = slice(base, base + win)
    q = jnp.concatenate([get_query(loc, 0) for loc in locs], axis=0)
    do = jnp.concatenate([get_query(loc, 1) for loc in locs], axis=0)
    q_all[lanes, :] = q

    def border(kind, half):
        parts = [get_border(loc, kind, side) for loc in locs[2 * half : 2 * half + 2] for side in range(2)]
        return jnp.concatenate(parts, axis=0)

    row = lax.broadcasted_iota(jnp.int32, (TOK, LANES), 0)
    lane = lax.broadcasted_iota(jnp.int32, (TOK, LANES), 1)
    group = lane // rows
    place = lane - group * rows + (xh * HALF if rows < TOK else 0)
    near = jnp.abs(place - row) <= window
    half_row = row % (2 * HALO)
    border_place = jnp.where(half_row < HALO, half_row - HALO, half_row + TOK - HALO)
    first = jnp.where(tile > 0, -HALO, 0)
    end = jnp.where(tile < 3, TOK + HALO, TOK)
    border_near = (jnp.abs(place - border_place) <= window) & (border_place >= first) & (border_place < end)
    row_group = row // (2 * HALO)

    k_borders = [border(0, half) for half in range(groups // 2)]
    v_borders = [border(1, half) for half in range(groups // 2)]
    top = None
    biases = []
    for b in range(n_blocks):
        keys = kcat[base + b * TOK : base + (b + 1) * TOK, :] if b < n_win else k_borders[b - n_win]
        s = dot_nt(keys, q)
        if b < groups - 1:
            s = jnp.where(group <= b, s, LOW)
        elif N_PAST <= b < n_win:
            s = jnp.where((group > b - N_PAST) | ((group == b - N_PAST) & near), s, LOW)
        elif b >= n_win:
            s = jnp.where(border_near & (row_group + 2 * (b - n_win) == group), s, LOW)
        s_ref[b * TOK : (b + 1) * TOK, :] = s
        here = jnp.max(s.reshape(TOK // 8, 8, LANES), axis=0) * scale
        bias = None
        if b < N_PAST and job * groups + b < N_LOC:
            bias = jnp.where(no_past, LOW, 0.0)
            here = here + bias
        top = here if top is None else jnp.maximum(top, here)
        biases.append(bias)
    top = jnp.max(top, axis=0, keepdims=True)
    total = jnp.zeros((8, LANES), F32)
    for b in range(n_blocks):
        shift = -top if biases[b] is None else biases[b] - top
        e = jnp.exp2(s_ref[b * TOK : (b + 1) * TOK, :] * scale + shift)
        total = total + jnp.sum(e.reshape(TOK // 8, 8, LANES), axis=0)
        if b < n_win:
            p_ref[base + b * TOK : base + (b + 1) * TOK, lanes] = e.astype(BF16)
        else:
            p_ref[CAT + (b - n_win) * TOK : CAT + (b - n_win + 1) * TOK, lanes] = e.astype(BF16)
    inverse = 1.0 / jnp.sum(total, axis=0, keepdims=True)
    do_t = (do.astype(F32).T * inverse).astype(BF16).astype(F32)
    do = do_t.T.astype(BF16)
    do_all[lanes, :] = do
    out_t = dot_nn(vtr[:, window_rows], p_ref[window_rows, lanes])
    for half in range(groups // 2):
        out_t = out_t + dot_nn(v_borders[half].T, p_ref[CAT + half * TOK : CAT + (half + 1) * TOK, lanes])
    out_b = (out_t * inverse).astype(BF16).astype(F32)
    delta = jnp.sum(out_b * do_t, axis=0, keepdims=True)
    out = out_b.T.astype(BF16)
    for g, loc in enumerate(locs):
        put_query(loc, 0, out[g * rows : (g + 1) * rows])
    for b in range(n_blocks):
        vals = vcat[base + b * TOK : base + (b + 1) * TOK, :] if b < n_win else v_borders[b - n_win]
        at = base + b * TOK if b < n_win else CAT + (b - n_win) * TOK
        ds = p_ref[at : at + TOK, lanes].astype(F32) * (dot_nt(vals, do) - delta)
        ds_ref[at : at + TOK, lanes] = ds.astype(BF16)
    dq_t = dot_nn(ktr[:, window_rows], ds_ref[window_rows, lanes])
    for half in range(groups // 2):
        dq_t = dq_t + dot_nn(k_borders[half].T, ds_ref[CAT + half * TOK : CAT + (half + 1) * TOK, lanes])
    dq = (dq_t * FACTOR).T.astype(BF16)
    for g, loc in enumerate(locs):
        put_query(loc, 1, dq[g * rows : (g + 1) * rows])
    for half in range(groups // 2):
        rows_at = slice(CAT + half * TOK, CAT + (half + 1) * TOK)
        dv_border = dot_nn(p_ref[rows_at, lanes], do).astype(BF16)
        dk_border = (dot_nn(ds_ref[rows_at, lanes], q) * FACTOR).astype(BF16)
        for kind, grad in enumerate((dk_border, dv_border)):
            for which, loc in enumerate(locs[2 * half : 2 * half + 2]):
                at = which * 2 * HALO
                put_border(loc, kind, grad[at : at + HALO], grad[at + HALO : at + 2 * HALO])


def keys_job(rows, put_past, put_own, q_all, do_all, p_ref, ds_ref):
    groups = LANES // rows
    jobs = N_LOC // groups
    for unit in range(CAT // UNIT):
        mine = [j for j in range(jobs) if j * groups // 2 <= unit < j * groups // 2 + (N_PAST + groups) // 2]
        lanes = slice(mine[0] * LANES, (mine[-1] + 1) * LANES)
        at = slice(unit * UNIT, (unit + 1) * UNIT)
        dk = dot_nn(ds_ref[at, lanes], q_all[lanes, :]) * FACTOR
        dv = dot_nn(p_ref[at, lanes], do_all[lanes, :])
        for kind, grad in enumerate((dk, dv)):
            for which in range(2):
                loc = unit * 2 + which
                part = grad[which * TOK : (which + 1) * TOK]
                if loc < N_LOC:
                    put_past(loc, kind, part.astype(BF16))
                else:
                    put_own(loc - N_LOC, kind, part.astype(BF16))


def load_keys(get_past, get_own, kcat, vcat, ktr, vtr):
    for kind, cat, tr in ((0, kcat, ktr), (1, vcat, vtr)):
        for loc in range(2 * N_LOC):
            block = get_past(loc, kind) if loc < N_LOC else get_own(loc - N_LOC, kind)
            cat[loc * TOK : (loc + 1) * TOK, :] = block
            tr[:, loc * TOK : (loc + 1) * TOK] = block.T


def attention_body(rows, window, no_past, get_past, get_own, get_query, get_border, put_query, put_border, put_past, put_own, *scratch):
    kcat, vcat, ktr, vtr, q_all, do_all, s0_ref, s1_ref, p_ref, ds_ref = scratch
    xh, tile = lax.axis_index("xh"), lax.axis_index("xl") * 2 + lax.axis_index("core")
    load_keys(get_past, get_own, kcat, vcat, ktr, vtr)
    for job in range(N_LOC * rows // LANES):
        queries_job(
            rows, job, window, no_past, xh, tile, get_query, get_border, put_query, put_border,
            kcat, vcat, ktr, vtr, q_all, do_all, s1_ref if job % 2 else s0_ref, p_ref, ds_ref,
        )
    keys_job(rows, put_past, put_own, q_all, do_all, p_ref, ds_ref)


def put_into(ref, *rest):
    def put(loc, kind, value):
        ref[(loc, kind, *rest)] = value

    return put


def attention_kernel(
    window_ref, kv_ref, past_ref, low_ref, high_ref, q_ref, o_ref, own_ref, back_ref, dlow_ref, dhigh_ref, *scratch
):
    y, xh = lax.axis_index("y"), lax.axis_index("xh")

    def put_border(loc, kind, low, high):
        dlow_ref[loc, kind, 0] = low
        dhigh_ref[loc, kind, 0] = high

    def slot_work(slot):
        rows = TOK if slot < FULL else HALF
        q_rows = slice(slot * TOK, slot * TOK + rows)

        def put_query(loc, kind, value):
            o_ref[loc, kind, q_rows] = value

        def put_past(loc, kind, value):
            o_ref[loc, kind, Q_ROWS:] = value

        attention_body(
            rows, window_ref[5 * y + (2 * xh + slot if slot < FULL else 4)], lax.axis_index("z") == 0,
            (lambda loc, kind: past_ref[loc, kind, 0]) if slot < FULL else (lambda loc, kind: q_ref[loc, kind, Q_ROWS:]),
            lambda loc, kind: kv_ref[loc, kind, 0],
            lambda loc, kind: q_ref[loc, kind, q_rows],
            lambda loc, kind, side: (high_ref if side else low_ref)[loc, kind, 0],
            put_query, put_border, put_into(back_ref, 0) if slot < FULL else put_past, put_into(own_ref, 0),
            *scratch,
        )

    for slot in range(SLOTS):
        pl.when(pl.program_id(0) == slot)(functools.partial(slot_work, slot))


SCRATCH = [
    pltpu.VMEM((CAT, DIM), BF16),
    pltpu.VMEM((CAT, DIM), BF16),
    pltpu.VMEM((DIM, CAT), BF16),
    pltpu.VMEM((DIM, CAT), BF16),
    pltpu.VMEM((N_LOC * TOK, DIM), BF16),
    pltpu.VMEM((N_LOC * TOK, DIM), BF16),
    pltpu.VMEM((14 * TOK, LANES), F32),
    pltpu.VMEM((14 * TOK, LANES), F32),
    pltpu.VMEM((CAT + UNIT, N_LOC * TOK), BF16),
    pltpu.VMEM((CAT + UNIT, N_LOC * TOK), BF16),
]
SMEM = pl.BlockSpec(memory_space=pltpu.SMEM)
ANYWHERE = pl.BlockSpec(memory_space=pl.ANY)
KV_SHAPE = (N_LOC, 2, SLOTS, TOK, DIM)
BORDER_SHAPE = (N_LOC, 2, SLOTS, HALO, DIM)
Q_SHAPE = (N_LOC, 2, ALL_ROWS, DIM)
PAIR_SHAPE = (N_LOC, 2, FULL, TOK, DIM)
RAW_SHAPE = (N_Y, 2, TOK, DIM)


def call(kernel, grid, in_specs, args, outs, flops=0, scratch=(), limit=60):
    moved = sum(a.size * a.dtype.itemsize for a in args) + sum(2 * math.prod(shape) for shape, _ in outs)
    return pl.pallas_call(
        kernel,
        grid=(grid,),
        out_shape=[jax.ShapeDtypeStruct(shape, BF16) for shape, _ in outs],
        in_specs=in_specs,
        out_specs=[spec for _, spec in outs],
        scratch_shapes=list(scratch),
        compiler_params=pltpu.CompilerParams(vmem_limit_bytes=limit * 2**20),
        cost_estimate=pl.CostEstimate(flops=flops, bytes_accessed=moved, transcendentals=0),
    )(*args)


def simple(kernel, args, outs, limit=32):
    return call(kernel, 1, [whole(a.shape) for a in args], args, [(o, whole(o)) for o in outs], limit=limit)


def by_slot(rows):
    return pl.BlockSpec((N_LOC, 2, 1, rows, DIM), lambda slot: (0, 0, slot, 0, 0))


def by_full_slot():
    return pl.BlockSpec((N_LOC, 2, 1, TOK, DIM), lambda slot: (0, 0, jnp.minimum(slot, FULL - 1), 0, 0))


def whole(shape):
    return pl.BlockSpec(shape, lambda _: (0,) * len(shape))


def split(shape, parts):
    return pl.BlockSpec((shape[0] // parts, *shape[1:]), lambda i: (i, *[0] * (len(shape) - 1)))


def attend(window, kv, past, low, high, qdo):
    specs = [SMEM, by_slot(TOK), by_full_slot(), by_slot(HALO), by_slot(HALO), whole(Q_SHAPE)]
    outs = [(Q_SHAPE, whole(Q_SHAPE)), (KV_SHAPE, by_slot(TOK)), (PAIR_SHAPE, by_full_slot())] + [(BORDER_SHAPE, by_slot(HALO))] * 2
    return call(attention_kernel, SLOTS, specs, (window, kv, past, low, high, qdo), outs, 10**10, SCRATCH, limit=ATTEND_MIB)


def exchange(x):
    return lax.all_to_all(x, PLACES, 0, 0)


def shards(queries, keys, values, cotangent, window):
    up = [(i, i + 1) for i in range(N_Z - 1)]
    down = [(i + 1, i) for i in range(N_Z - 1)]
    packed_kv, raw = simple(pack_keys_kernel, (keys, values), [KV_SHAPE, RAW_SHAPE])
    raw = lax.ppermute(raw, "z", up)
    (packed_q,) = simple(pack_queries_kernel, (queries, cotangent, raw), [Q_SHAPE])
    kv = exchange(packed_kv)
    past = lax.ppermute(kv[:, :, :FULL], "z", up)
    low = lax.ppermute(kv[:, :, :, TOK - HALO :], TILES, up)
    high = lax.ppermute(kv[:, :, :, :HALO], TILES, down)
    qdo = exchange(packed_q)
    odq, own, back, dlow, dhigh = attend(window, kv, past, low, high, qdo)
    got = lax.ppermute(back, "z", down)
    from_high = lax.ppermute(dlow, TILES, down)
    from_low = lax.ppermute(dhigh, TILES, up)
    out_q = exchange(odq)
    args = (own, got, from_low, from_high)
    outs = [(KV_SHAPE, split(KV_SHAPE, 4))]
    (merged,) = call(merge_kernel, 4, [split(a.shape, 4) for a in args], args, outs, limit=32)
    out_kv = exchange(merged)
    attended, grad_queries, raw = simple(unpack_queries_kernel, (out_q,), [queries.shape, queries.shape, RAW_SHAPE])
    raw = lax.ppermute(raw, "z", down)
    grad_keys, grad_values = simple(unpack_keys_kernel, (out_kv, raw), [keys.shape] * 2)
    return attended, grad_queries, grad_keys, grad_values


def solution(mesh):
    fine = Mesh(mesh.devices.reshape(N_Z, N_Y, N_X, 2, 2), AXES)
    rows = P(AXES, None)
    return jax.shard_map(
        shards,
        mesh=fine,
        in_specs=(rows, rows, rows, rows, P()),
        out_specs=(rows, rows, rows, rows),
        check_vma=False,
    )
```

```python
import functools
import math

import jax
import jax.numpy as jnp
from jax import lax
from jax.experimental import pallas as pl
from jax.experimental.pallas import tpu as pltpu
from jax.sharding import Mesh, PartitionSpec as P

HEADS = 20
DIM = 128
TOK = 128
HALO = 32
N_Z, N_Y, N_X = 4, 4, 2
N_LOC = N_Y * N_X
FULL = 2
SLOTS = 3
HALF = TOK // 2
PAST_ROWS = slice(2 * TOK, 3 * TOK)
SHARED_ROWS = slice(3 * TOK, 3 * TOK + HALF)
ALL_ROWS = 3 * TOK + HALF
LOW = -1.0e30
FACTOR = DIM ** -0.5
LOG2E = 1.4426950408889634
ATTEND_MIB = 60
AXES = ("z", "y", "xh", "xl", "core")
PLACES = ("y", "xh")
TILES = ("xl", "core")
F32 = jnp.float32
BF16 = jnp.bfloat16


def head_cols(place, slot):
    head = place // N_X * 5 + (place % N_X * 2 + slot if slot < FULL else 4)
    return slice(head * DIM, (head + 1) * DIM)


def pack_keys_kernel(k_ref, v_ref, kv_ref, raw_ref):
    for y in range(N_Y):
        raw_ref[y, 0] = k_ref[:, head_cols(y * N_X, FULL)]
        raw_ref[y, 1] = v_ref[:, head_cols(y * N_X, FULL)]
    for place in range(N_LOC):
        for kind, ref in enumerate((k_ref, v_ref)):
            for slot in range(SLOTS):
                kv_ref[place, kind, slot] = ref[:, head_cols(place, slot)]


def pack_queries_kernel(q_ref, do_ref, raw_ref, qdo_ref):
    for place in range(N_LOC):
        start = place % N_X * HALF
        for kind, ref in enumerate((q_ref, do_ref)):
            for slot in range(FULL):
                qdo_ref[place, kind, slot * TOK : (slot + 1) * TOK] = ref[:, head_cols(place, slot)]
            qdo_ref[place, kind, SHARED_ROWS] = ref[start : start + HALF, head_cols(place, FULL)]
            qdo_ref[place, kind, PAST_ROWS] = raw_ref[place // N_X, kind]


def unpack_queries_kernel(odq_ref, o_ref, dq_ref, raw_ref):
    for place in range(N_LOC):
        start = place % N_X * HALF
        for kind, ref in enumerate((o_ref, dq_ref)):
            for slot in range(FULL):
                ref[:, head_cols(place, slot)] = odq_ref[place, kind, slot * TOK : (slot + 1) * TOK]
            ref[start : start + HALF, head_cols(place, FULL)] = odq_ref[place, kind, SHARED_ROWS]
    for kind in range(2):
        for y in range(N_Y):
            first, second = odq_ref[y * N_X, kind, PAST_ROWS], odq_ref[y * N_X + 1, kind, PAST_ROWS]
            raw_ref[y, kind] = (first.astype(F32) + second.astype(F32)).astype(BF16)


def unpack_keys_kernel(grads_ref, raw_ref, dk_ref, dv_ref):
    for kind, ref in enumerate((dk_ref, dv_ref)):
        for place in range(N_LOC):
            for slot in range(FULL):
                ref[:, head_cols(place, slot)] = grads_ref[place, kind, slot]
        for place in range(0, N_LOC, N_X):
            both = grads_ref[place, kind, FULL].astype(F32) + grads_ref[place + 1, kind, FULL].astype(F32)
            both = both + raw_ref[place // N_X, kind].astype(F32)
            ref[:, head_cols(place, FULL)] = both.astype(BF16)


def merge_kernel(own_ref, got_ref, from_low_ref, from_high_ref, out_ref):
    for loc in range(own_ref.shape[0]):
        for kind in range(2):
            for slot in range(SLOTS):
                at = (loc, kind, slot)
                total = own_ref[at].astype(F32)
                if slot < FULL:
                    total = total + got_ref[at].astype(F32)
                first = total[:HALO] + from_low_ref[at].astype(F32)
                last = total[TOK - HALO :] + from_high_ref[at].astype(F32)
                out_ref[loc, kind, slot, :HALO] = first.astype(BF16)
                out_ref[loc, kind, slot, HALO : TOK - HALO] = total[HALO : TOK - HALO].astype(BF16)
                out_ref[loc, kind, slot, TOK - HALO :] = last.astype(BF16)


def dot_nt(a, b):
    return lax.dot_general(a, b, (((1,), (1,)), ((), ())), preferred_element_type=F32)


def dot_nn(a, b):
    return lax.dot_general(a, b, (((1,), (0,)), ((), ())), preferred_element_type=F32)


LANES = 2 * TOK
UNIT = 2 * TOK
CAT = 2 * N_LOC * TOK
N_PAST = 8
N_PHASES = 5


def queries_job(
    rows, job, window, no_past, xh, tile, get_query, get_border, put_query, put_border,
    kcat, vcat, ktr, vtr, q_all, do_all, s_ref, p_ref, ds_ref,
):
    groups = LANES // rows
    n_win = N_PAST + groups
    n_blocks = n_win + groups // 2
    win = n_win * TOK
    base = job * groups * TOK
    locs = [job * groups + g for g in range(groups)]
    lanes = slice(job * LANES, (job + 1) * LANES)
    scale = FACTOR * LOG2E
    window_rows = slice(base, base + win)
    q = jnp.concatenate([get_query(loc, 0) for loc in locs], axis=0)
    do = jnp.concatenate([get_query(loc, 1) for loc in locs], axis=0)
    q_all[lanes, :] = q

    def border(kind, half):
        parts = [get_border(loc, kind, side) for loc in locs[2 * half : 2 * half + 2] for side in range(2)]
        return jnp.concatenate(parts, axis=0)

    row = lax.broadcasted_iota(jnp.int32, (TOK, LANES), 0)
    lane = lax.broadcasted_iota(jnp.int32, (TOK, LANES), 1)
    group = lane // rows
    place = lane - group * rows + (xh * HALF if rows < TOK else 0)
    near = jnp.abs(place - row) <= window
    half_row = row % (2 * HALO)
    border_place = jnp.where(half_row < HALO, half_row - HALO, half_row + TOK - HALO)
    first = jnp.where(tile > 0, -HALO, 0)
    end = jnp.where(tile < 3, TOK + HALO, TOK)
    border_near = (jnp.abs(place - border_place) <= window) & (border_place >= first) & (border_place < end)
    row_group = row // (2 * HALO)

    k_borders = [border(0, half) for half in range(groups // 2)]
    v_borders = [border(1, half) for half in range(groups // 2)]
    top = None
    biases = []
    for b in range(n_blocks):
        keys = kcat[base + b * TOK : base + (b + 1) * TOK, :] if b < n_win else k_borders[b - n_win]
        s = dot_nt(keys, q)
        if b < groups - 1:
            s = jnp.where(group <= b, s, LOW)
        elif N_PAST <= b < n_win:
            s = jnp.where((group > b - N_PAST) | ((group == b - N_PAST) & near), s, LOW)
        elif b >= n_win:
            s = jnp.where(border_near & (row_group + 2 * (b - n_win) == group), s, LOW)
        s_ref[b * TOK : (b + 1) * TOK, :] = s
        here = jnp.max(s.reshape(TOK // 8, 8, LANES), axis=0) * scale
        bias = None
        if b < N_PAST and job * groups + b < N_LOC:
            bias = jnp.where(no_past, LOW, 0.0)
            here = here + bias
        top = here if top is None else jnp.maximum(top, here)
        biases.append(bias)
    yield
    top = jnp.max(top, axis=0, keepdims=True)
    total = jnp.zeros((8, LANES), F32)
    for b in range(n_blocks):
        shift = -top if biases[b] is None else biases[b] - top
        e = jnp.exp2(s_ref[b * TOK : (b + 1) * TOK, :] * scale + shift)
        total = total + jnp.sum(e.reshape(TOK // 8, 8, LANES), axis=0)
        if b < n_win:
            p_ref[base + b * TOK : base + (b + 1) * TOK, lanes] = e.astype(BF16)
        else:
            p_ref[CAT + (b - n_win) * TOK : CAT + (b - n_win + 1) * TOK, lanes] = e.astype(BF16)
    inverse = 1.0 / jnp.sum(total, axis=0, keepdims=True)
    do_t = (do.astype(F32).T * inverse).astype(BF16).astype(F32)
    do = do_t.T.astype(BF16)
    do_all[lanes, :] = do
    yield
    out_t = dot_nn(vtr[:, window_rows], p_ref[window_rows, lanes])
    for half in range(groups // 2):
        out_t = out_t + dot_nn(v_borders[half].T, p_ref[CAT + half * TOK : CAT + (half + 1) * TOK, lanes])
    out_b = (out_t * inverse).astype(BF16).astype(F32)
    delta = jnp.sum(out_b * do_t, axis=0, keepdims=True)
    out = out_b.T.astype(BF16)
    for g, loc in enumerate(locs):
        put_query(loc, 0, out[g * rows : (g + 1) * rows])
    yield
    for b in range(n_blocks):
        vals = vcat[base + b * TOK : base + (b + 1) * TOK, :] if b < n_win else v_borders[b - n_win]
        at = base + b * TOK if b < n_win else CAT + (b - n_win) * TOK
        ds = p_ref[at : at + TOK, lanes].astype(F32) * (dot_nt(vals, do) - delta)
        ds_ref[at : at + TOK, lanes] = ds.astype(BF16)
    yield
    dq_t = dot_nn(ktr[:, window_rows], ds_ref[window_rows, lanes])
    for half in range(groups // 2):
        dq_t = dq_t + dot_nn(k_borders[half].T, ds_ref[CAT + half * TOK : CAT + (half + 1) * TOK, lanes])
    dq = (dq_t * FACTOR).T.astype(BF16)
    for g, loc in enumerate(locs):
        put_query(loc, 1, dq[g * rows : (g + 1) * rows])
    for half in range(groups // 2):
        rows_at = slice(CAT + half * TOK, CAT + (half + 1) * TOK)
        dv_border = dot_nn(p_ref[rows_at, lanes], do).astype(BF16)
        dk_border = (dot_nn(ds_ref[rows_at, lanes], q) * FACTOR).astype(BF16)
        for kind, grad in enumerate((dk_border, dv_border)):
            for which, loc in enumerate(locs[2 * half : 2 * half + 2]):
                at = which * 2 * HALO
                put_border(loc, kind, grad[at : at + HALO], grad[at + HALO : at + 2 * HALO])
    yield


def keys_job(rows, put_past, put_own, q_all, do_all, p_ref, ds_ref):
    groups = LANES // rows
    jobs = N_LOC // groups
    for unit in range(CAT // UNIT):
        mine = [j for j in range(jobs) if j * groups // 2 <= unit < j * groups // 2 + (N_PAST + groups) // 2]
        lanes = slice(mine[0] * LANES, (mine[-1] + 1) * LANES)
        at = slice(unit * UNIT, (unit + 1) * UNIT)
        dk = dot_nn(ds_ref[at, lanes], q_all[lanes, :]) * FACTOR
        dv = dot_nn(p_ref[at, lanes], do_all[lanes, :])
        for kind, grad in enumerate((dk, dv)):
            for which in range(2):
                loc = unit * 2 + which
                part = grad[which * TOK : (which + 1) * TOK]
                if loc < N_LOC:
                    put_past(loc, kind, part.astype(BF16))
                else:
                    put_own(loc - N_LOC, kind, part.astype(BF16))


def load_keys(get_past, get_own, kcat, vcat, ktr, vtr):
    for kind, cat, tr in ((0, kcat, ktr), (1, vcat, vtr)):
        for loc in range(2 * N_LOC):
            block = get_past(loc, kind) if loc < N_LOC else get_own(loc - N_LOC, kind)
            cat[loc * TOK : (loc + 1) * TOK, :] = block
            tr[:, loc * TOK : (loc + 1) * TOK] = block.T


def attention_body(rows, window, no_past, get_past, get_own, get_query, get_border, put_query, put_border, put_past, put_own, *scratch):
    kcat, vcat, ktr, vtr, q_all, do_all, s0_ref, s1_ref, p_ref, ds_ref = scratch
    xh, tile = lax.axis_index("xh"), lax.axis_index("xl") * 2 + lax.axis_index("core")
    load_keys(get_past, get_own, kcat, vcat, ktr, vtr)
    jobs = [
        queries_job(
            rows, job, window, no_past, xh, tile, get_query, get_border, put_query, put_border,
            kcat, vcat, ktr, vtr, q_all, do_all, s1_ref if job % 2 else s0_ref, p_ref, ds_ref,
        )
        for job in range(N_LOC * rows // LANES)
    ]
    for step in range(N_PHASES + len(jobs) - 1):
        for at, job in reversed(list(enumerate(jobs))):
            if 0 <= step - at < N_PHASES:
                next(job)
    keys_job(rows, put_past, put_own, q_all, do_all, p_ref, ds_ref)


def put_into(ref, *rest):
    def put(loc, kind, value):
        ref[(loc, kind, *rest)] = value

    return put


def attention_kernel(
    window_ref, kv_ref, past_ref, low_ref, high_ref, q_ref, past2_ref, q2_ref,
    o_out, own_ref, back_ref, dlow_ref, dhigh_ref, o_ref, sems, *scratch,
):
    y, xh = lax.axis_index("y"), lax.axis_index("xh")

    def put_border(loc, kind, low, high):
        dlow_ref[loc, kind, 0] = low
        dhigh_ref[loc, kind, 0] = high

    def moves(rows, first):
        return [
            pltpu.make_async_copy(o_ref.at[:, kind, rows], o_out.at[:, kind, rows], sems.at[first + kind])
            for kind in range(2)
        ]

    parts = (slice(0, TOK), slice(TOK, 2 * TOK), PAST_ROWS, SHARED_ROWS)

    def slot_work(slot):
        rows = TOK if slot < FULL else HALF
        q_rows = parts[slot] if slot < FULL else SHARED_ROWS

        def put_query(loc, kind, value):
            o_ref[loc, kind, q_rows] = value

        def put_past(loc, kind, value):
            o_ref[loc, kind, PAST_ROWS] = value

        attention_body(
            rows, window_ref[5 * y + (2 * xh + slot if slot < FULL else 4)], lax.axis_index("z") == 0,
            (lambda loc, kind: past_ref[loc, kind, 0]) if slot < FULL else (lambda loc, kind: past2_ref[loc, kind]),
            lambda loc, kind: kv_ref[loc, kind, 0],
            lambda loc, kind: (q_ref if slot < FULL else q2_ref)[loc, kind],
            lambda loc, kind, side: (high_ref if side else low_ref)[loc, kind, 0],
            put_query, put_border, put_into(back_ref, 0) if slot < FULL else put_past, put_into(own_ref, 0),
            *scratch,
        )
        mine = [slot] if slot < FULL else [2, 3]
        for part in mine:
            for move in moves(parts[part], 2 * part):
                move.start()
        if slot == FULL:
            for part in range(4):
                for move in moves(parts[part], 2 * part):
                    move.wait()

    for slot in range(SLOTS):
        pl.when(pl.program_id(0) == slot)(functools.partial(slot_work, slot))


SCRATCH = [
    pltpu.VMEM((CAT, DIM), BF16),
    pltpu.VMEM((CAT, DIM), BF16),
    pltpu.VMEM((DIM, CAT), BF16),
    pltpu.VMEM((DIM, CAT), BF16),
    pltpu.VMEM((N_LOC * TOK, DIM), BF16),
    pltpu.VMEM((N_LOC * TOK, DIM), BF16),
    pltpu.VMEM((14 * TOK, LANES), F32),
    pltpu.VMEM((14 * TOK, LANES), F32),
    pltpu.VMEM((CAT + UNIT, N_LOC * TOK), BF16),
    pltpu.VMEM((CAT + UNIT, N_LOC * TOK), BF16),
]
SMEM = pl.BlockSpec(memory_space=pltpu.SMEM)
ANYWHERE = pl.BlockSpec(memory_space=pl.ANY)
KV_SHAPE = (N_LOC, 2, SLOTS, TOK, DIM)
BORDER_SHAPE = (N_LOC, 2, SLOTS, HALO, DIM)
Q_SHAPE = (N_LOC, 2, ALL_ROWS, DIM)
PAIR_SHAPE = (N_LOC, 2, FULL, TOK, DIM)
RAW_SHAPE = (N_Y, 2, TOK, DIM)


def call(kernel, grid, in_specs, args, outs, flops=0, scratch=(), limit=60):
    moved = sum(a.size * a.dtype.itemsize for a in args) + sum(2 * math.prod(shape) for shape, _ in outs)
    return pl.pallas_call(
        kernel,
        grid=(grid,),
        out_shape=[jax.ShapeDtypeStruct(shape, BF16) for shape, _ in outs],
        in_specs=in_specs,
        out_specs=[spec for _, spec in outs],
        scratch_shapes=list(scratch),
        compiler_params=pltpu.CompilerParams(vmem_limit_bytes=limit * 2**20),
        cost_estimate=pl.CostEstimate(flops=flops, bytes_accessed=moved, transcendentals=0),
    )(*args)


def simple(kernel, args, outs, limit=32):
    return call(kernel, 1, [whole(a.shape) for a in args], args, [(o, whole(o)) for o in outs], limit=limit)


def by_slot(rows):
    return pl.BlockSpec((N_LOC, 2, 1, rows, DIM), lambda slot: (0, 0, slot, 0, 0))


def by_full_slot():
    return pl.BlockSpec((N_LOC, 2, 1, TOK, DIM), lambda slot: (0, 0, jnp.minimum(slot, FULL - 1), 0, 0))


def whole(shape):
    return pl.BlockSpec(shape, lambda _: (0,) * len(shape))


def split(shape, parts):
    return pl.BlockSpec((shape[0] // parts, *shape[1:]), lambda i: (i, *[0] * (len(shape) - 1)))


def attend(window, kv, past, low, high, qdo):
    q_spec = pl.BlockSpec((N_LOC, 2, TOK, DIM), lambda slot: (0, 0, jnp.minimum(slot, FULL - 1), 0))
    past2_spec = pl.BlockSpec((N_LOC, 2, TOK, DIM), lambda slot: (0, 0, 2, 0))
    q2_spec = pl.BlockSpec((N_LOC, 2, HALF, DIM), lambda slot: (0, 0, 6, 0))
    specs = [SMEM, by_slot(TOK), by_full_slot(), by_slot(HALO), by_slot(HALO), q_spec, past2_spec, q2_spec]
    outs = [(Q_SHAPE, ANYWHERE), (KV_SHAPE, by_slot(TOK)), (PAIR_SHAPE, by_full_slot())]
    outs += [(BORDER_SHAPE, by_slot(HALO))] * 2
    scratch = [pltpu.VMEM(Q_SHAPE, BF16), pltpu.SemaphoreType.DMA((8,)), *SCRATCH]
    args = (window, kv, past, low, high, qdo, qdo, qdo)
    return call(attention_kernel, SLOTS, specs, args, outs, 10**10, scratch, limit=ATTEND_MIB)


def exchange(x):
    return lax.all_to_all(x, PLACES, 0, 0)


def shards(queries, keys, values, cotangent, window):
    up = [(i, i + 1) for i in range(N_Z - 1)]
    down = [(i + 1, i) for i in range(N_Z - 1)]
    packed_kv, raw = simple(pack_keys_kernel, (keys, values), [KV_SHAPE, RAW_SHAPE], limit=60)
    raw = lax.ppermute(raw, "z", up)
    (packed_q,) = simple(pack_queries_kernel, (queries, cotangent, raw), [Q_SHAPE])
    kv = exchange(packed_kv)
    past = lax.ppermute(kv[:, :, :FULL], "z", up)
    low = lax.ppermute(kv[:, :, :, TOK - HALO :], TILES, up)
    high = lax.ppermute(kv[:, :, :, :HALO], TILES, down)
    qdo = exchange(packed_q)
    odq, own, back, dlow, dhigh = attend(window, kv, past, low, high, qdo)
    got = lax.ppermute(back, "z", down)
    from_high = lax.ppermute(dlow, TILES, down)
    from_low = lax.ppermute(dhigh, TILES, up)
    out_q = exchange(odq)
    args = (own, got, from_low, from_high)
    outs = [(KV_SHAPE, split(KV_SHAPE, 4))]
    (merged,) = call(merge_kernel, 4, [split(a.shape, 4) for a in args], args, outs, limit=32)
    out_kv = exchange(merged)
    attended, grad_queries, raw = simple(unpack_queries_kernel, (out_q,), [queries.shape, queries.shape, RAW_SHAPE])
    raw = lax.ppermute(raw, "z", down)
    grad_keys, grad_values = simple(unpack_keys_kernel, (out_kv, raw), [keys.shape] * 2)
    return attended, grad_queries, grad_keys, grad_values


def solution(mesh):
    fine = Mesh(mesh.devices.reshape(N_Z, N_Y, N_X, 2, 2), AXES)
    rows = P(AXES, None)
    return jax.shard_map(
        shards,
        mesh=fine,
        in_specs=(rows, rows, rows, rows, P()),
        out_specs=(rows, rows, rows, rows),
        check_vma=False,
    )
```

```python
import functools
import math

import jax
import jax.numpy as jnp
from jax import lax
from jax.experimental import pallas as pl
from jax.experimental.pallas import tpu as pltpu
from jax.sharding import Mesh, PartitionSpec as P

HEADS = 20
DIM = 128
TOK = 128
HALO = 32
N_Z, N_Y, N_X = 4, 4, 2
N_LOC = N_Y * N_X
FULL = 2
SLOTS = 3
HALF = TOK // 2
PAST_ROWS = slice(2 * TOK, 3 * TOK)
SHARED_ROWS = slice(3 * TOK, 3 * TOK + HALF)
ALL_ROWS = 3 * TOK + HALF
LOW = -1.0e30
FACTOR = DIM ** -0.5
LOG2E = 1.4426950408889634
ATTEND_MIB = 60
AXES = ("z", "y", "xh", "xl", "core")
PLACES = ("y", "xh")
TILES = ("xl", "core")
F32 = jnp.float32
BF16 = jnp.bfloat16


def head_cols(place, slot):
    head = place // N_X * 5 + (place % N_X * 2 + slot if slot < FULL else 4)
    return slice(head * DIM, (head + 1) * DIM)


def pack_keys_kernel(k_ref, v_ref, kv_ref, raw_ref):
    for y in range(N_Y):
        raw_ref[y, 0] = k_ref[:, head_cols(y * N_X, FULL)]
        raw_ref[y, 1] = v_ref[:, head_cols(y * N_X, FULL)]
    for place in range(N_LOC):
        for kind, ref in enumerate((k_ref, v_ref)):
            for slot in range(SLOTS):
                kv_ref[place, kind, slot] = ref[:, head_cols(place, slot)]


def pack_queries_kernel(q_ref, do_ref, raw_ref, qdo_ref):
    for place in range(N_LOC):
        start = place % N_X * HALF
        for kind, ref in enumerate((q_ref, do_ref)):
            for slot in range(FULL):
                qdo_ref[place, kind, slot * TOK : (slot + 1) * TOK] = ref[:, head_cols(place, slot)]
            qdo_ref[place, kind, SHARED_ROWS] = ref[start : start + HALF, head_cols(place, FULL)]
            qdo_ref[place, kind, PAST_ROWS] = raw_ref[place // N_X, kind]


def unpack_queries_kernel(odq_ref, o_ref, dq_ref, raw_ref):
    for place in range(N_LOC):
        start = place % N_X * HALF
        for kind, ref in enumerate((o_ref, dq_ref)):
            for slot in range(FULL):
                ref[:, head_cols(place, slot)] = odq_ref[place, kind, slot * TOK : (slot + 1) * TOK]
            ref[start : start + HALF, head_cols(place, FULL)] = odq_ref[place, kind, SHARED_ROWS]
    for kind in range(2):
        for y in range(N_Y):
            first, second = odq_ref[y * N_X, kind, PAST_ROWS], odq_ref[y * N_X + 1, kind, PAST_ROWS]
            raw_ref[y, kind] = (first.astype(F32) + second.astype(F32)).astype(BF16)


def unpack_keys_kernel(grads_ref, raw_ref, dk_ref, dv_ref):
    for kind, ref in enumerate((dk_ref, dv_ref)):
        for place in range(N_LOC):
            for slot in range(FULL):
                ref[:, head_cols(place, slot)] = grads_ref[place, kind, slot]
        for place in range(0, N_LOC, N_X):
            both = grads_ref[place, kind, FULL].astype(F32) + grads_ref[place + 1, kind, FULL].astype(F32)
            both = both + raw_ref[place // N_X, kind].astype(F32)
            ref[:, head_cols(place, FULL)] = both.astype(BF16)


def merge_kernel(own_ref, got_ref, from_low_ref, from_high_ref, out_ref):
    for loc in range(own_ref.shape[0]):
        for kind in range(2):
            for slot in range(SLOTS):
                at = (loc, kind, slot)
                total = own_ref[at].astype(F32)
                if slot < FULL:
                    total = total + got_ref[at].astype(F32)
                first = total[:HALO] + from_low_ref[at].astype(F32)
                last = total[TOK - HALO :] + from_high_ref[at].astype(F32)
                out_ref[loc, kind, slot, :HALO] = first.astype(BF16)
                out_ref[loc, kind, slot, HALO : TOK - HALO] = total[HALO : TOK - HALO].astype(BF16)
                out_ref[loc, kind, slot, TOK - HALO :] = last.astype(BF16)


def dot_nt(a, b):
    return lax.dot_general(a, b, (((1,), (1,)), ((), ())), preferred_element_type=F32)


def dot_nn(a, b):
    return lax.dot_general(a, b, (((1,), (0,)), ((), ())), preferred_element_type=F32)


LANES = 2 * TOK
UNIT = 2 * TOK
CAT = 2 * N_LOC * TOK
N_PAST = 8
N_PHASES = 5


def queries_job(
    rows, job, window, no_past, xh, tile, get_query, get_border, put_query, put_border,
    kcat, vcat, ktr, vtr, q_all, do_all, s_ref, p_ref, ds_ref,
):
    groups = LANES // rows
    n_win = N_PAST + groups
    n_blocks = n_win + groups // 2
    win = n_win * TOK
    base = job * groups * TOK
    locs = [job * groups + g for g in range(groups)]
    lanes = slice(job * LANES, (job + 1) * LANES)
    scale = FACTOR * LOG2E
    window_rows = slice(base, base + win)
    q = jnp.concatenate([get_query(loc, 0) for loc in locs], axis=0)
    do = jnp.concatenate([get_query(loc, 1) for loc in locs], axis=0)
    q_all[lanes, :] = q

    def border(kind, half):
        parts = [get_border(loc, kind, side) for loc in locs[2 * half : 2 * half + 2] for side in range(2)]
        return jnp.concatenate(parts, axis=0)

    row = lax.broadcasted_iota(jnp.int32, (TOK, LANES), 0)
    lane = lax.broadcasted_iota(jnp.int32, (TOK, LANES), 1)
    group = lane // rows
    place = lane - group * rows + (xh * HALF if rows < TOK else 0)
    near = jnp.abs(place - row) <= window
    half_row = row % (2 * HALO)
    border_place = jnp.where(half_row < HALO, half_row - HALO, half_row + TOK - HALO)
    first = jnp.where(tile > 0, -HALO, 0)
    end = jnp.where(tile < 3, TOK + HALO, TOK)
    border_near = (jnp.abs(place - border_place) <= window) & (border_place >= first) & (border_place < end)
    row_group = row // (2 * HALO)

    k_borders = [border(0, half) for half in range(groups // 2)]
    v_borders = [border(1, half) for half in range(groups // 2)]
    top = None
    biases = []
    for b in range(n_blocks):
        keys = kcat[base + b * TOK : base + (b + 1) * TOK, :] if b < n_win else k_borders[b - n_win]
        s = dot_nt(keys, q)
        if b < groups - 1:
            s = jnp.where(group <= b, s, LOW)
        elif N_PAST <= b < n_win:
            s = jnp.where((group > b - N_PAST) | ((group == b - N_PAST) & near), s, LOW)
        elif b >= n_win:
            s = jnp.where(border_near & (row_group + 2 * (b - n_win) == group), s, LOW)
        s_ref[b * TOK : (b + 1) * TOK, :] = s
        here = jnp.max(s.reshape(TOK // 8, 8, LANES), axis=0) * scale
        bias = None
        if b < N_PAST and job * groups + b < N_LOC:
            bias = jnp.where(no_past, LOW, 0.0)
            here = here + bias
        top = here if top is None else jnp.maximum(top, here)
        biases.append(bias)
    yield
    top = jnp.max(top, axis=0, keepdims=True)
    total = jnp.zeros((8, LANES), F32)
    for b in range(n_blocks):
        shift = -top if biases[b] is None else biases[b] - top
        e = jnp.exp2(s_ref[b * TOK : (b + 1) * TOK, :] * scale + shift)
        total = total + jnp.sum(e.reshape(TOK // 8, 8, LANES), axis=0)
        if b < n_win:
            p_ref[base + b * TOK : base + (b + 1) * TOK, lanes] = e.astype(BF16)
        else:
            p_ref[CAT + (b - n_win) * TOK : CAT + (b - n_win + 1) * TOK, lanes] = e.astype(BF16)
    inverse = 1.0 / jnp.sum(total, axis=0, keepdims=True)
    do_t = (do.astype(F32).T * inverse).astype(BF16).astype(F32)
    do = do_t.T.astype(BF16)
    do_all[lanes, :] = do
    yield
    out_t = dot_nn(vtr[:, window_rows], p_ref[window_rows, lanes])
    for half in range(groups // 2):
        out_t = out_t + dot_nn(v_borders[half].T, p_ref[CAT + half * TOK : CAT + (half + 1) * TOK, lanes])
    out_b = (out_t * inverse).astype(BF16).astype(F32)
    delta = jnp.sum(out_b * do_t, axis=0, keepdims=True)
    out = out_b.T.astype(BF16)
    for g, loc in enumerate(locs):
        put_query(loc, 0, out[g * rows : (g + 1) * rows])
    yield
    for b in range(n_blocks):
        vals = vcat[base + b * TOK : base + (b + 1) * TOK, :] if b < n_win else v_borders[b - n_win]
        at = base + b * TOK if b < n_win else CAT + (b - n_win) * TOK
        ds = p_ref[at : at + TOK, lanes].astype(F32) * (dot_nt(vals, do) - delta)
        ds_ref[at : at + TOK, lanes] = ds.astype(BF16)
    yield
    dq_t = dot_nn(ktr[:, window_rows], ds_ref[window_rows, lanes])
    for half in range(groups // 2):
        dq_t = dq_t + dot_nn(k_borders[half].T, ds_ref[CAT + half * TOK : CAT + (half + 1) * TOK, lanes])
    dq = (dq_t * FACTOR).T.astype(BF16)
    for g, loc in enumerate(locs):
        put_query(loc, 1, dq[g * rows : (g + 1) * rows])
    for half in range(groups // 2):
        rows_at = slice(CAT + half * TOK, CAT + (half + 1) * TOK)
        dv_border = dot_nn(p_ref[rows_at, lanes], do).astype(BF16)
        dk_border = (dot_nn(ds_ref[rows_at, lanes], q) * FACTOR).astype(BF16)
        for kind, grad in enumerate((dk_border, dv_border)):
            for which, loc in enumerate(locs[2 * half : 2 * half + 2]):
                at = which * 2 * HALO
                put_border(loc, kind, grad[at : at + HALO], grad[at + HALO : at + 2 * HALO])
    yield


def keys_job(rows, put_past, put_own, q_all, do_all, p_ref, ds_ref):
    groups = LANES // rows
    jobs = N_LOC // groups
    for unit in range(CAT // UNIT):
        mine = [j for j in range(jobs) if j * groups // 2 <= unit < j * groups // 2 + (N_PAST + groups) // 2]
        lanes = slice(mine[0] * LANES, (mine[-1] + 1) * LANES)
        at = slice(unit * UNIT, (unit + 1) * UNIT)
        dk = dot_nn(ds_ref[at, lanes], q_all[lanes, :]) * FACTOR
        dv = dot_nn(p_ref[at, lanes], do_all[lanes, :])
        for kind, grad in enumerate((dk, dv)):
            for which in range(2):
                loc = unit * 2 + which
                part = grad[which * TOK : (which + 1) * TOK]
                if loc < N_LOC:
                    put_past(loc, kind, part.astype(BF16))
                else:
                    put_own(loc - N_LOC, kind, part.astype(BF16))


def load_keys(get_past, get_own, kcat, vcat, ktr, vtr):
    for kind, cat, tr in ((0, kcat, ktr), (1, vcat, vtr)):
        for loc in range(2 * N_LOC):
            block = get_past(loc, kind) if loc < N_LOC else get_own(loc - N_LOC, kind)
            cat[loc * TOK : (loc + 1) * TOK, :] = block
            tr[:, loc * TOK : (loc + 1) * TOK] = block.T


def attention_body(rows, window, no_past, get_past, get_own, get_query, get_border, put_query, put_border, put_past, put_own, *scratch):
    kcat, vcat, ktr, vtr, q_all, do_all, s0_ref, s1_ref, p_ref, ds_ref = scratch
    xh, tile = lax.axis_index("xh"), lax.axis_index("xl") * 2 + lax.axis_index("core")
    load_keys(get_past, get_own, kcat, vcat, ktr, vtr)
    jobs = [
        queries_job(
            rows, job, window, no_past, xh, tile, get_query, get_border, put_query, put_border,
            kcat, vcat, ktr, vtr, q_all, do_all, s1_ref if job % 2 else s0_ref, p_ref, ds_ref,
        )
        for job in range(N_LOC * rows // LANES)
    ]
    for step in range(N_PHASES + len(jobs) - 1):
        for at, job in reversed(list(enumerate(jobs))):
            if 0 <= step - at < N_PHASES:
                next(job)
    keys_job(rows, put_past, put_own, q_all, do_all, p_ref, ds_ref)


def put_into(ref, *rest):
    def put(loc, kind, value):
        ref[(loc, kind, *rest)] = value

    return put


def attention_kernel(
    window_ref, kv_ref, past_ref, low_ref, high_ref, q_ref, past2_ref, q2_ref,
    o_out, own_ref, back_ref, dlow_ref, dhigh_ref, o_ref, sems, *scratch,
):
    y, xh = lax.axis_index("y"), lax.axis_index("xh")

    def put_border(loc, kind, low, high):
        dlow_ref[loc, kind, 0] = low
        dhigh_ref[loc, kind, 0] = high

    def moves(rows, first):
        return [
            pltpu.make_async_copy(o_ref.at[:, kind, rows], o_out.at[:, kind, rows], sems.at[first + kind])
            for kind in range(2)
        ]

    parts = (slice(0, TOK), slice(TOK, 2 * TOK), PAST_ROWS, SHARED_ROWS)

    def slot_work(slot):
        rows = TOK if slot < FULL else HALF
        q_rows = parts[slot] if slot < FULL else SHARED_ROWS

        def put_query(loc, kind, value):
            o_ref[loc, kind, q_rows] = value

        def put_past(loc, kind, value):
            o_ref[loc, kind, PAST_ROWS] = value

        attention_body(
            rows, window_ref[5 * y + (2 * xh + slot if slot < FULL else 4)], lax.axis_index("z") == 0,
            (lambda loc, kind: past_ref[loc, kind, 0]) if slot < FULL else (lambda loc, kind: past2_ref[loc, kind]),
            lambda loc, kind: kv_ref[loc, kind, 0],
            lambda loc, kind: (q_ref if slot < FULL else q2_ref)[loc, kind],
            lambda loc, kind, side: (high_ref if side else low_ref)[loc, kind, 0],
            put_query, put_border, put_into(back_ref, 0) if slot < FULL else put_past, put_into(own_ref, 0),
            *scratch,
        )
        mine = [slot] if slot < FULL else [2, 3]
        for part in mine:
            for move in moves(parts[part], 2 * part):
                move.start()
        if slot == FULL:
            for part in range(4):
                for move in moves(parts[part], 2 * part):
                    move.wait()

    for slot in range(SLOTS):
        pl.when(pl.program_id(0) == slot)(functools.partial(slot_work, slot))


SCRATCH = [
    pltpu.VMEM((CAT, DIM), BF16),
    pltpu.VMEM((CAT, DIM), BF16),
    pltpu.VMEM((DIM, CAT), BF16),
    pltpu.VMEM((DIM, CAT), BF16),
    pltpu.VMEM((N_LOC * TOK, DIM), BF16),
    pltpu.VMEM((N_LOC * TOK, DIM), BF16),
    pltpu.VMEM((14 * TOK, LANES), F32),
    pltpu.VMEM((14 * TOK, LANES), F32),
    pltpu.VMEM((CAT + UNIT, N_LOC * TOK), BF16),
    pltpu.VMEM((CAT + UNIT, N_LOC * TOK), BF16),
]
SMEM = pl.BlockSpec(memory_space=pltpu.SMEM)
ANYWHERE = pl.BlockSpec(memory_space=pl.ANY)
KV_SHAPE = (N_LOC, 2, SLOTS, TOK, DIM)
BORDER_SHAPE = (N_LOC, 2, SLOTS, HALO, DIM)
Q_SHAPE = (N_LOC, 2, ALL_ROWS, DIM)
PAIR_SHAPE = (N_LOC, 2, FULL, TOK, DIM)
RAW_SHAPE = (N_Y, 2, TOK, DIM)


def call(kernel, grid, in_specs, args, outs, flops=0, scratch=(), limit=60):
    moved = sum(a.size * a.dtype.itemsize for a in args) + sum(2 * math.prod(shape) for shape, _ in outs)
    return pl.pallas_call(
        kernel,
        grid=(grid,),
        out_shape=[jax.ShapeDtypeStruct(shape, BF16) for shape, _ in outs],
        in_specs=in_specs,
        out_specs=[spec for _, spec in outs],
        scratch_shapes=list(scratch),
        compiler_params=pltpu.CompilerParams(vmem_limit_bytes=limit * 2**20),
        cost_estimate=pl.CostEstimate(flops=flops, bytes_accessed=moved, transcendentals=0),
    )(*args)


def simple(kernel, args, outs, limit=32):
    return call(kernel, 1, [whole(a.shape) for a in args], args, [(o, whole(o)) for o in outs], limit=limit)


def by_slot(rows):
    return pl.BlockSpec((N_LOC, 2, 1, rows, DIM), lambda slot: (0, 0, slot, 0, 0))


def by_full_slot():
    return pl.BlockSpec((N_LOC, 2, 1, TOK, DIM), lambda slot: (0, 0, jnp.minimum(slot, FULL - 1), 0, 0))


def whole(shape):
    return pl.BlockSpec(shape, lambda _: (0,) * len(shape))


def split(shape, parts):
    return pl.BlockSpec((shape[0] // parts, *shape[1:]), lambda i: (i, *[0] * (len(shape) - 1)))


def attend(window, kv, past, low, high, qdo):
    q_spec = pl.BlockSpec((N_LOC, 2, TOK, DIM), lambda slot: (0, 0, jnp.minimum(slot, FULL - 1), 0))
    past2_spec = pl.BlockSpec((N_LOC, 2, TOK, DIM), lambda slot: (0, 0, 2, 0))
    q2_spec = pl.BlockSpec((N_LOC, 2, HALF, DIM), lambda slot: (0, 0, 6, 0))
    specs = [SMEM, by_slot(TOK), by_full_slot(), by_slot(HALO), by_slot(HALO), q_spec, past2_spec, q2_spec]
    outs = [(Q_SHAPE, ANYWHERE), (KV_SHAPE, by_slot(TOK)), (PAIR_SHAPE, by_full_slot())]
    outs += [(BORDER_SHAPE, by_slot(HALO))] * 2
    scratch = [pltpu.VMEM(Q_SHAPE, BF16), pltpu.SemaphoreType.DMA((8,)), *SCRATCH]
    args = (window, kv, past, low, high, qdo, qdo, qdo)
    return call(attention_kernel, SLOTS, specs, args, outs, 10**10, scratch, limit=ATTEND_MIB)


def exchange(x):
    return lax.all_to_all(x, PLACES, 0, 0)


def shards(queries, keys, values, cotangent, window):
    up = [(i, i + 1) for i in range(N_Z - 1)]
    down = [(i + 1, i) for i in range(N_Z - 1)]
    packed_kv, raw = simple(pack_keys_kernel, (keys, values), [KV_SHAPE, RAW_SHAPE], limit=60)
    raw = lax.ppermute(raw, "z", up)
    (packed_q,) = simple(pack_queries_kernel, (queries, cotangent, raw), [Q_SHAPE])
    kv = exchange(packed_kv)
    past = lax.ppermute(kv[:, :, :FULL], "z", up)
    low = lax.ppermute(kv[:, :, :, TOK - HALO :], TILES, up)
    high = lax.ppermute(kv[:, :, :, :HALO], TILES, down)
    qdo = exchange(packed_q)
    odq, own, back, dlow, dhigh = attend(window, kv, past, low, high, qdo)
    got = lax.ppermute(back, "z", down)
    from_high = lax.ppermute(dlow, TILES, down)
    from_low = lax.ppermute(dhigh, TILES, up)
    out_q = exchange(odq)
    args = (own, got, from_low, from_high)
    outs = [(KV_SHAPE, split(KV_SHAPE, 4))]
    (merged,) = call(merge_kernel, 4, [split(a.shape, 4) for a in args], args, outs, 8 * 10**9, limit=32)
    out_kv = exchange(merged)
    attended, grad_queries, raw = simple(unpack_queries_kernel, (out_q,), [queries.shape, queries.shape, RAW_SHAPE])
    raw = lax.ppermute(raw, "z", down)
    grad_keys, grad_values = simple(unpack_keys_kernel, (out_kv, raw), [keys.shape] * 2)
    return attended, grad_queries, grad_keys, grad_values


def solution(mesh):
    fine = Mesh(mesh.devices.reshape(N_Z, N_Y, N_X, 2, 2), AXES)
    rows = P(AXES, None)
    return jax.shard_map(
        shards,
        mesh=fine,
        in_specs=(rows, rows, rows, rows, P()),
        out_specs=(rows, rows, rows, rows),
        check_vma=False,
    )
```
